512 devices in a mesh: leaf: 128 (over z, y, core), rhs: 4 (over x).
Axes of the slice: x: 4, y: 8, z: 8, core: 2. Of those that a mesh axis runs over, the one named last changes fastest.
Arguments:
- leaf_shift: float32 [256, 262144], P('rhs', 'leaf'), may hold values from -6 to 6
- sep_shift: float32 [256, 4096], P('rhs', 'leaf'), may hold values from -6 to 6
- leaf_noise: float32 [256, 262144], P('rhs', 'leaf'), may hold values from -6 to 6
- sep_noise: float32 [256, 4096], P('rhs', 'leaf'), may hold values from -6 to 6
- leaf_inverse: float32 [2048, 128, 128], P('leaf'), may hold values from -1 to 2, as said below
- leaf_panel: float32 [2048, 64, 128], P('leaf'), may hold values from -0.0625 to 0.0625
- panel_blocks: int32 [2048, 8], P('leaf'), may hold values from 0 to 239, as said below
- sep_inverse: float32 [1024, 1920], P('leaf', 'rhs'), may hold values from -1 to 2, as said below
- sep_coupling: float32 [1024, 4352], P('leaf', 'rhs'), may hold values from -0.125 to 0.125
Outputs:
- leaf_sample: float32 [256, 262144], P('rhs', 'leaf')
- sep_sample: float32 [256, 4096], P('rhs', 'leaf')
The draws below stay inside these ranges and needn't reach their ends.
Inputs may be any that keep to these rules, and one draw needn't show every extreme that they name: `leaf_inverse`: each [128, 128] block is lower triangular with a positive diagonal. `sep_inverse`: in the column block of depth k (columns O_k to O_k + S_k - 1), row p has zeros beyond column O_k + (p mod S_k) and a positive entry there: each separator's inverse is lower triangular. `panel_blocks`: the 8 numbers of a row are different.
All inputs are finite; a program needn't handle non-finite values.
Results may differ from the reference program's by a relative error of at most 0.00015.
Values sent between devices are 32-bit elements; how exact they have to be, the bound alone decides.
No kernel may reach another device: no remote copies, remote signals or barrier semaphores. Data moves between devices by JAX's collectives and lax.ppermute only.
A program may use at most 64 MiB of HBM per device.

```python
import math
import jax
import jax.numpy as jnp
from jax import lax

TILE = 128
SEP_DEV = 8
LEVELS = 4
NB = 8
NODES = 16
RHS = 256
S0 = 1024
ANC = 1920
COUPLED = 4352
LEAFCOLS = 262144
SEPCOLS = 4096
N_LEAF = 128


def draw_leaf_inverse(key, part):
    key_diag, key_below = jax.random.split(jax.random.fold_in(key, 11))
    full_shape = (N_LEAF * NODES, TILE, TILE)
    below_part = jnp.clip(jax.random.normal(key_below, full_shape, jnp.float32), -4.0, 4.0)
    diag_part = jnp.exp(jax.random.uniform(key_diag, full_shape, jnp.float32, math.log(0.5), math.log(2.0)))
    row_index = jnp.arange(TILE, dtype=jnp.int32)[:, None]
    column = jnp.arange(TILE, dtype=jnp.int32)[None, :]
    scaled = below_part * (0.5 * TILE ** (-0.5))
    return jnp.where(column < row_index, scaled, jnp.where(column == row_index, diag_part, 0.0)).astype(jnp.float32)


def draw_sep_inverse(key, part):
    key_diag, key_below = jax.random.split(jax.random.fold_in(key, 23))
    row_count = N_LEAF * SEP_DEV
    full_shape = (row_count, ANC)
    offsets = [0]
    for height in range(LEVELS):
        offsets.append(offsets[-1] + (S0 >> height))
    column = jnp.arange(ANC, dtype=jnp.int32)[None, :]
    row_index = jnp.arange(row_count, dtype=jnp.int32)[:, None]
    level_of = jnp.zeros(column.shape, jnp.int32)
    for height in range(1, LEVELS):
        level_of = level_of + (column >= offsets[height]).astype(jnp.int32)
    start_of = jnp.zeros(column.shape, jnp.int32)
    size_of = jnp.ones(column.shape, jnp.int32)
    for height in range(LEVELS):
        start_of = jnp.where(level_of == height, offsets[height], start_of)
        size_of = jnp.where(level_of == height, S0 >> height, size_of)
    within = column - start_of
    own_place = row_index % size_of
    below_part = jnp.clip(jax.random.normal(key_below, full_shape, jnp.float32), -4.0, 4.0)
    diag_part = jnp.exp(jax.random.uniform(key_diag, full_shape, jnp.float32, math.log(0.5), math.log(2.0)))
    scale_of = 0.5 * size_of.astype(jnp.float32) ** (-0.5)
    return jnp.where(within < own_place, below_part * scale_of, jnp.where(within == own_place, diag_part, 0.0)).astype(jnp.float32)


def draw_panel_blocks(key, part):
    row_total = N_LEAF * NODES
    block_count = ANC // SEP_DEV
    scores = jax.random.randint(jax.random.fold_in(key, 37), (row_total, block_count), 0, 1 << 20)
    distinct = scores * block_count + jnp.arange(block_count, dtype=jnp.int32)[None, :]
    ranked = jnp.argsort(distinct, axis=1)
    return ranked[:, :NB].astype(jnp.int32)


def steps_of(stream_key, shape, cuts, smallest, top_value):
    def one(dim, blocks):
        steps = jax.random.uniform(jax.random.fold_in(jax.random.fold_in(stream_key, 6), dim), (blocks,), jnp.float32, smallest / len(cuts), top_value / len(cuts))
        return jnp.repeat(jnp.exp(steps), shape[dim] // blocks).reshape((-1,) + (1,) * (len(shape) - dim - 1))

    loudness = one(*cuts[0])
    for cut in cuts[1:]:
        loudness = loudness * one(*cut)
    return loudness


def bell_draw(rng, dims, spread, bound, cuts=(), kind=jnp.bfloat16):
    values = jax.random.normal(rng, dims, jnp.float32) * spread
    if len(cuts) > 0:
        values = steps_of(rng, dims, cuts, -0.22, 0.18) * values
    return jnp.clip(values, min=-bound, max=bound).astype(kind)


def setup_inputs(seed: int = 0) -> dict:
    key_list = jax.random.split(jax.random.key(seed), 10)
    return {
        "leaf_shift": bell_draw(key_list[0], (RHS, LEAFCOLS), 1.0, 6.0, ((0, 4), (1, 128)), jnp.float32),
        "sep_shift": bell_draw(key_list[1], (RHS, SEPCOLS), 1.0, 6.0, ((0, 4), (1, 128)), jnp.float32),
        "leaf_noise": bell_draw(key_list[2], (RHS, LEAFCOLS), 1.0, 6.0, ((0, 4), (1, 128)), jnp.float32),
        "sep_noise": bell_draw(key_list[3], (RHS, SEPCOLS), 1.0, 6.0, ((0, 4), (1, 128)), jnp.float32),
        "leaf_inverse": draw_leaf_inverse(jax.random.fold_in(key_list[9], 71), 0),
        "leaf_panel": bell_draw(key_list[5], (N_LEAF * NODES, NB * SEP_DEV, TILE), (TILE * NB * NODES // 2) ** -0.5, 0.0625, ((0, 128),), jnp.float32),
        "panel_blocks": draw_panel_blocks(jax.random.fold_in(key_list[9], 71), 0),
        "sep_inverse": draw_sep_inverse(jax.random.fold_in(key_list[9], 71), 0),
        "sep_coupling": bell_draw(key_list[8], (N_LEAF * SEP_DEV, COUPLED), (2 * S0) ** -0.5, 0.125, ((0, 128), (1, 4)), jnp.float32),
    }


exact_mode = lax.Precision.HIGHEST


def reference(leaf_shift, sep_shift, leaf_noise, sep_noise, leaf_inverse, leaf_panel, panel_blocks, sep_inverse, sep_coupling):
    samples = leaf_shift.shape[0]
    starts = [0]
    for height in range(LEVELS):
        starts.append(starts[-1] + (S0 >> height))
    segment_at = [0]
    for height in range(1, LEVELS):
        segment_at.append(segment_at[-1] + starts[height])
    leaf_total = N_LEAF * NODES
    node_device = (jnp.arange(leaf_total, dtype=jnp.int32) // NODES)[:, None]
    level_of = jnp.zeros(panel_blocks.shape, jnp.int32)
    for height in range(1, LEVELS):
        level_of = level_of + (panel_blocks >= starts[height] // SEP_DEV).astype(jnp.int32)
    block_start = jnp.array([starts[h] // SEP_DEV for h in range(LEVELS)], dtype=jnp.int32)[level_of]
    cube_of = jnp.array([N_LEAF >> h for h in range(LEVELS)], dtype=jnp.int32)[level_of]
    piece_ids = (level_of * N_LEAF + (node_device // cube_of) * cube_of + panel_blocks - block_start).astype(jnp.int32)

    shifted = leaf_shift.reshape(samples, leaf_total, TILE)
    leaf_forward = jnp.einsum("rnt,nct->rnc", shifted, leaf_inverse, precision=exact_mode)
    pieces = jnp.einsum("rnc,nkc->rnk", leaf_forward, leaf_panel, precision=exact_mode)
    flattened = jnp.transpose(pieces.reshape(samples, leaf_total * NB, SEP_DEV), (1, 0, 2)).reshape(leaf_total * NB, samples * SEP_DEV)
    summed = jax.ops.segment_sum(flattened, piece_ids.reshape(-1), num_segments=LEVELS * N_LEAF)
    levels_update = jnp.transpose(summed.reshape(LEVELS, N_LEAF, samples, SEP_DEV), (0, 2, 1, 3)).reshape(LEVELS, samples, N_LEAF * SEP_DEV)

    shift_levels = sep_shift.reshape(samples, N_LEAF, LEVELS, SEP_DEV)
    noise_levels = sep_noise.reshape(samples, N_LEAF, LEVELS, SEP_DEV)
    coupling_sums = [jnp.zeros((samples, N_LEAF * SEP_DEV), jnp.float32) for height in range(LEVELS)]
    forward_levels = [None] * LEVELS
    for height in reversed(range(LEVELS)):
        sep_count = 2 ** height
        sep_size = S0 >> height
        residual = shift_levels[:, :, height, :].reshape(samples, N_LEAF * SEP_DEV) - levels_update[height] - coupling_sums[height]
        inverse_block = sep_inverse[:, starts[height]:starts[height] + sep_size].reshape(sep_count, sep_size, sep_size)
        solved = jnp.einsum("rqc,qgc->rqg", residual.reshape(samples, sep_count, sep_size), inverse_block, precision=exact_mode)
        solved = solved.reshape(samples, N_LEAF * SEP_DEV)
        forward_levels[height] = solved
        for ancestor in range(height):
            count_up = 2 ** ancestor
            size_up = S0 >> ancestor
            cube_up = N_LEAF >> ancestor
            begin = segment_at[height - 1] + starts[ancestor]
            couple_block = sep_coupling[:, begin:begin + size_up].reshape(count_up, cube_up, SEP_DEV, size_up)
            added = jnp.einsum("rqei,qeih->rqh", solved.reshape(samples, count_up, cube_up, SEP_DEV), couple_block, precision=exact_mode)
            coupling_sums[ancestor] = coupling_sums[ancestor] + added.reshape(samples, N_LEAF * SEP_DEV)

    result_levels = [None] * LEVELS
    for height in range(LEVELS):
        sep_count = 2 ** height
        sep_size = S0 >> height
        lifted = forward_levels[height] + noise_levels[:, :, height, :].reshape(samples, N_LEAF * SEP_DEV)
        for ancestor in range(height):
            count_up = 2 ** ancestor
            size_up = S0 >> ancestor
            cube_up = N_LEAF >> ancestor
            begin = segment_at[height - 1] + starts[ancestor]
            couple_block = sep_coupling[:, begin:begin + size_up].reshape(count_up, cube_up, SEP_DEV, size_up)
            taken = jnp.einsum("rqh,qeih->rqei", result_levels[ancestor].reshape(samples, count_up, size_up), couple_block, precision=exact_mode)
            lifted = lifted - taken.reshape(samples, N_LEAF * SEP_DEV)
        inverse_block = sep_inverse[:, starts[height]:starts[height] + sep_size].reshape(sep_count, sep_size, sep_size)
        solution = jnp.einsum("rqg,qgc->rqc", lifted.reshape(samples, sep_count, sep_size), inverse_block, precision=exact_mode)
        result_levels[height] = solution.reshape(samples, N_LEAF * SEP_DEV)

    sep_sample = jnp.stack([level.reshape(samples, N_LEAF, SEP_DEV) for level in result_levels], axis=2).reshape(samples, N_LEAF * LEVELS * SEP_DEV)
    joined = jnp.concatenate(result_levels, axis=1)
    take_index = (piece_ids * SEP_DEV)[:, :, None] + jnp.arange(SEP_DEV, dtype=jnp.int32)[None, None, :]
    picked = jnp.take(joined, take_index.reshape(-1), axis=1).reshape(samples, leaf_total, NB * SEP_DEV)
    leaf_lifted = leaf_forward + leaf_noise.reshape(samples, leaf_total, TILE)
    leaf_lifted = leaf_lifted - jnp.einsum("rnk,nkc->rnc", picked, leaf_panel, precision=exact_mode)
    leaf_sample = jnp.einsum("rnt,ntc->rnc", leaf_lifted, leaf_inverse, precision=exact_mode).reshape(samples, leaf_total * TILE)
    return leaf_sample, sep_sample
```

```python
import jax
import jax.numpy as jnp
from jax import lax
from jax.sharding import Mesh, PartitionSpec as P

SEP_DEV = 8
LEVELS = 4
NB = 8
S0 = 1024
ANC = 1920
PLANE = 16
STARTS = (0, 1024, 1536, 1792, 1920)
SEG = (0, 0, 1024, 2560)

exact = lax.Precision.HIGHEST


def ein(spec, a, b):
    return jnp.einsum(spec, a, b, precision=exact)


def body(
    leaf_shift,
    sep_shift,
    leaf_noise,
    sep_noise,
    leaf_inverse,
    leaf_panel,
    panel_blocks,
    sep_inverse,
    sep_coupling,
):
    yc = ("y", "core")
    zz = ("zh", "zq")
    samples = leaf_shift.shape[0]
    nodes, tile = leaf_inverse.shape[0], leaf_inverse.shape[1]
    group = samples // PLANE
    zq = lax.axis_index("zq")
    zh = lax.axis_index("zh")
    z = zh * 4 + zq
    dev = z * PLANE + lax.axis_index("y") * 2 + lax.axis_index("core")

    own = jnp.concatenate([sep_inverse, sep_coupling], axis=1)
    quad = lax.all_gather(own, ("zq", "rhs"), axis=0, tiled=False).reshape(4, 4, 8, 1568)
    quad = jnp.transpose(quad, (0, 2, 1, 3))
    inv = quad[..., :480].reshape(4, 8, 1920)
    cou = quad[..., 480:].reshape(4, 8, 4352)
    l1 = jnp.concatenate([inv[..., 1024:1536], cou[..., :1024]], axis=2)
    l2 = jnp.concatenate([inv[..., 1536:1792], cou[..., 1024:2560]], axis=2)
    l2 = lax.dynamic_slice_in_dim(l2, zq // 2 * 2, 2, 0)
    l3 = jnp.concatenate([inv[..., 1792:], cou[..., 2560:]], axis=2)
    l3 = lax.dynamic_slice_in_dim(l3, zq, 1, 0)
    l0 = lax.dynamic_slice_in_dim(inv[..., :1024], zq, 1, 0)
    flat = lambda m: jnp.transpose(m, (1, 0, 2)).reshape(8, -1)
    packed = jnp.concatenate([flat(l1), flat(l2), flat(l3), flat(l0)], axis=1)
    path = lax.all_gather(packed, yc, axis=0, tiled=True)
    f1 = path[:, :6144].reshape(512, 1536)
    f2 = path[:, 6144:9728].reshape(256, 1792)
    f3 = path[:, 9728:11648]
    f0 = path[:, 11648:]

    selector = (
        panel_blocks[:, :, None] == jnp.arange(ANC // 8, dtype=jnp.int32)[None, None, :]
    ).astype(jnp.float32)
    shifted = leaf_shift.reshape(samples, nodes, tile)
    leaf_forward = ein("rnt,nct->rnc", shifted, leaf_inverse)
    pieces = ein("rnc,nkc->rnk", leaf_forward, leaf_panel).reshape(samples, nodes, NB, SEP_DEV)
    update = ein("rnbi,nba->rai", pieces, selector).reshape(samples, ANC)
    part = -update
    sep_own = sep_shift.reshape(samples, LEVELS, SEP_DEV)
    for k in range(LEVELS):
        at = STARTS[k] + dev % (128 >> k) * SEP_DEV
        cur = lax.dynamic_slice_in_dim(part, at, SEP_DEV, 1)
        part = lax.dynamic_update_slice_in_dim(part, cur + sep_own[:, k, :], at, 1)
    pay = jnp.concatenate([part, sep_noise, jnp.zeros((samples, 96), jnp.float32)], axis=1)
    pay = lax.all_to_all(pay.reshape(PLANE, group, 2048), yc, 0, 0)
    v = jnp.sum(pay[..., :ANC], axis=0)
    noise = pay[..., ANC : ANC + 32].reshape(PLANE, group, LEVELS, SEP_DEV)
    noise = jnp.transpose(noise, (2, 1, 0, 3)).reshape(LEVELS, group, 128)

    g3 = ein("rc,gc->rg", v[:, 1792:], f3[:, :128])
    w = v[:, :1792] - ein("rg,gc->rc", g3, f3[:, 128:])
    g2 = ein("rc,gc->rg", w[:, 1536:], f2[:, :256])
    w = w[:, :1536] - ein("rg,gc->rc", g2, f2[:, 256:])
    g1 = ein("rc,gc->rg", w[:, 1024:], f1[:, :512])
    w = w[:, :1024] - ein("rg,gc->rc", g1, f1[:, 512:])
    mask1 = (jnp.arange(4) == zq).astype(jnp.float32)
    mask2 = (jnp.arange(2) == zq % 2).astype(jnp.float32)
    g1 = g1 + (noise[1][:, :, None] * mask1).reshape(group, 512)
    g2 = g2 + (noise[2][:, :, None] * mask2).reshape(group, 256)
    send = jnp.concatenate([w, g1, g2], axis=1)
    got = lax.all_to_all(jnp.broadcast_to(send, (8,) + send.shape), zz, 0, 0)
    r0 = jnp.sum(got[..., :1024], axis=0)
    in_quad = (jnp.arange(8) // 4 == zh).astype(jnp.float32)[:, None, None]
    in_pair = (jnp.arange(8) // 2 == z // 2).astype(jnp.float32)[:, None, None]
    g1 = jnp.sum(got[..., 1024:1536] * in_quad, axis=0)
    g2 = jnp.sum(got[..., 1536:] * in_pair, axis=0)

    y0 = ein("rc,gc->rg", r0, f0) + noise[0]
    x0p = ein("rg,gc->rc", y0, f0)
    x0 = jnp.sum(lax.all_to_all(jnp.broadcast_to(x0p, (8,) + x0p.shape), zz, 0, 0), axis=0)
    y1 = g1 - ein("rc,gc->rg", x0, f1[:, 512:])
    x1 = ein("rg,gc->rc", y1, f1[:, :512])
    x = jnp.concatenate([x0, x1], axis=1)
    y2 = g2 - ein("rc,gc->rg", x, f2[:, 256:])
    x2 = ein("rg,gc->rc", y2, f2[:, :256])
    x = jnp.concatenate([x, x2], axis=1)
    y3 = g3 + noise[3] - ein("rc,gc->rg", x, f3[:, 128:])
    x3 = ein("rg,gc->rc", y3, f3[:, :128])
    x = jnp.concatenate([x, x3], axis=1)
    gathered = lax.all_gather(x, yc, axis=0, tiled=True)

    sep_out = jnp.concatenate(
        [
            lax.dynamic_slice_in_dim(gathered, STARTS[k] + dev % (128 >> k) * SEP_DEV, SEP_DEV, 1)
            for k in range(LEVELS)
        ],
        axis=1,
    )
    blocks_view = gathered.reshape(samples, ANC // 8, SEP_DEV)
    picked = ein("rai,nba->rnbi", blocks_view, selector).reshape(samples, nodes, NB * SEP_DEV)
    lifted = leaf_forward + leaf_noise.reshape(samples, nodes, tile)
    lifted = lifted - ein("rnk,nkc->rnc", picked, leaf_panel)
    leaf_out = ein("rnt,ntc->rnc", lifted, leaf_inverse).reshape(samples, nodes * tile)
    return leaf_out, sep_out


def solution(mesh):
    inner = Mesh(mesh.devices.reshape(2, 4, 8, 2, 4), ("zh", "zq", "y", "core", "rhs"))
    leaf = ("zh", "zq", "y", "core")
    data = P("rhs", leaf)
    rows = P(leaf, "rhs")
    return jax.shard_map(
        body,
        mesh=inner,
        in_specs=(data, data, data, data, P(leaf), P(leaf), P(leaf), rows, rows),
        out_specs=(data, data),
        check_vma=False,
    )
```

```python
import jax
import jax.numpy as jnp
from jax import lax
from jax.experimental import pallas as pl
from jax.experimental.pallas import tpu as pltpu
from jax.sharding import Mesh, PartitionSpec as P

SEP_DEV = 8
LEVELS = 4
NB = 8
ANC = 1920
PLANE = 16
GROUP = 4
SAMPLES = 64
NODES = 16
TILE = 128
STARTS = (0, 1024, 1536, 1792, 1920)
L2_AT = 6144
L3_AT = 9728
L0_AT = 11648
PACK = 12672

exact = lax.Precision.HIGHEST
VMEM_LIMIT = 48 * 1024 * 1024


def nn(a, b):
    return lax.dot_general(a, b, (((1,), (0,)), ((), ())), precision=exact, preferred_element_type=jnp.float32)


def nt(a, b):
    return lax.dot_general(a, b, (((1,), (1,)), ((), ())), precision=exact, preferred_element_type=jnp.float32)


def tn(a, b):
    return lax.dot_general(a, b, (((0,), (0,)), ((), ())), precision=exact, preferred_element_type=jnp.float32)


def vspec(n):
    return [pl.BlockSpec(memory_space=pltpu.VMEM)] * n


def call(kernel, outs, ins, smem=0, scratch=(), flops=0, nbytes=0):
    many = isinstance(outs, (list, tuple))
    return pl.pallas_call(
        kernel,
        out_shape=outs,
        in_specs=[pl.BlockSpec(memory_space=pltpu.SMEM)] * smem + vspec(len(ins) - smem),
        out_specs=tuple(vspec(len(outs))) if many else vspec(1)[0],
        scratch_shapes=list(scratch),
        compiler_params=pltpu.CompilerParams(vmem_limit_bytes=VMEM_LIMIT),
        cost_estimate=pl.CostEstimate(flops=flops, bytes_accessed=nbytes, transcendentals=0),
    )(*ins)


def f32(*shape):
    return jax.ShapeDtypeStruct(shape, jnp.float32)


def leaf_forward_kernel(blocks, at, shift, sep_t, sep_noise, inverse, panel, lf_out, pay_out, acc):
    acc[...] = jnp.zeros_like(acc)

    def step(n, carry):
        cols = pl.ds(pl.multiple_of(n * TILE, TILE), TILE)
        lf = nt(shift[:, cols], inverse[n])
        lf_out[:, cols] = lf
        pieces = nt(panel[n], lf)
        for b in range(NB):
            rows = pl.ds(pl.multiple_of(blocks[n, b] * SEP_DEV, SEP_DEV), SEP_DEV)
            acc[rows, :] = acc[rows, :] - pieces[b * SEP_DEV : (b + 1) * SEP_DEV, :]
        return carry

    lax.fori_loop(0, NODES, step, 0)
    for k in range(LEVELS):
        rows = pl.ds(pl.multiple_of(at[k], SEP_DEV), SEP_DEV)
        acc[rows, :] = acc[rows, :] + sep_t[k * SEP_DEV : (k + 1) * SEP_DEV, :]
    for c in range(ANC // TILE):
        pay_out[:, c * TILE : (c + 1) * TILE] = acc[c * TILE : (c + 1) * TILE, :].T
    pay_out[:, ANC:] = sep_noise[...]


def leaf_prepare_kernel(lf, noise, inverse, panel, base_out, w_out):
    def step(n, carry):
        cols = pl.ds(pl.multiple_of(n * TILE, TILE), TILE)
        base_out[:, cols] = nn(lf[:, cols] + noise[:, cols], inverse[n])
        w_out[n] = nn(panel[n], inverse[n])
        return carry

    lax.fori_loop(0, NODES, step, 0)


def forward_kernel(place, v, noise, path, send_out, g3_out):
    w = v[...]
    g3 = nt(w[:, 1792:], path[:, L3_AT : L3_AT + 128])
    w = w[:, :1792] - nn(g3, path[:, L3_AT + 128 : L0_AT])
    g3_out[...] = g3 + noise[3]
    zq = place[0]
    two = []
    r2 = w[:, 1536:]
    w = w[:, :1536]
    for p in range(2):
        at = L2_AT + p * 1792
        g = nt(r2, path[:, at : at + 256])
        w = w - nn(g, path[:, at + 256 : at + 1792])
        two.append(g + jnp.where(zq % 2 == p, noise[2], 0.0))
    r1 = w[:, 1024:]
    w = w[:, :1024]
    one = []
    for q in range(4):
        at = q * 1536
        g = nt(r1, path[:, at : at + 512])
        w = w - nn(g, path[:, at + 512 : at + 1536])
        one.append(g + jnp.where(zq == q, noise[1], 0.0))
    for d in range(8):
        send_out[d, :, :1024] = w
        for q in range(4):
            send_out[d, :, 1024 + q * 128 : 1152 + q * 128] = one[q]
        for p in range(2):
            send_out[d, :, 1536 + p * 128 : 1664 + p * 128] = two[p]


def top_kernel(got, noise, path, send_out):
    r0 = got[0, :, :1024]
    for d in range(1, 8):
        r0 = r0 + got[d, :, :1024]
    y0 = nt(r0, path[...]) + noise[0]
    x0 = nn(y0, path[...])
    for d in range(8):
        send_out[d] = x0


def backward_kernel(place, got, got0, g3, path, x_out):
    x0 = got0[0]
    for d in range(1, 8):
        x0 = x0 + got0[d]
    x_out[:, :1024] = x0
    z = place[0] + 4 * place[1]
    g1 = jnp.zeros((GROUP, 512), jnp.float32)
    g2 = jnp.zeros((GROUP, 256), jnp.float32)
    for d in range(8):
        g1 = g1 + jnp.where(z // 4 == d // 4, got[d, :, 1024:1536], 0.0)
        g2 = g2 + jnp.where(z // 2 == d // 2, got[d, :, 1536:], 0.0)
    x1 = jnp.zeros((GROUP, 512), jnp.float32)
    for q in range(4):
        at = q * 1536
        y = g1[:, q * 128 : (q + 1) * 128] - nt(x0, path[:, at + 512 : at + 1536])
        x1 = x1 + nn(y, path[:, at : at + 512])
    x_out[:, 1024:1536] = x1
    x2 = jnp.zeros((GROUP, 256), jnp.float32)
    for p in range(2):
        at = L2_AT + p * 1792
        y = g2[:, p * 128 : (p + 1) * 128] - nt(x_out[:, :1536], path[:, at + 256 : at + 1792])
        x2 = x2 + nn(y, path[:, at : at + 256])
    x_out[:, 1536:1792] = x2
    y = g3[...] - nt(x_out[:, :1792], path[:, L3_AT + 128 : L0_AT])
    x_out[:, 1792:] = nn(y, path[:, L3_AT : L3_AT + 128])


def leaf_backward_kernel(blocks, at, x, base, w, leaf_out, sep_out, rows_s, cols_s):
    for g in range(PLANE):
        rows_s[g * GROUP : (g + 1) * GROUP, :] = x[g]
    for c in range(ANC // TILE):
        cols_s[c * TILE : (c + 1) * TILE, :] = rows_s[:, c * TILE : (c + 1) * TILE].T
    for k in range(LEVELS):
        rows = pl.ds(pl.multiple_of(at[k], SEP_DEV), SEP_DEV)
        sep_out[k * SEP_DEV : (k + 1) * SEP_DEV, :] = cols_s[rows, :]

    def step(n, carry):
        cols = pl.ds(pl.multiple_of(n * TILE, TILE), TILE)
        picked = jnp.concatenate(
            [cols_s[pl.ds(pl.multiple_of(blocks[n, b] * SEP_DEV, SEP_DEV), SEP_DEV), :] for b in range(NB)],
            axis=0,
        )
        leaf_out[:, cols] = base[:, cols] - tn(picked, w[n])
        return carry

    lax.fori_loop(0, NODES, step, 0)


def body(
    leaf_shift,
    sep_shift,
    leaf_noise,
    sep_noise,
    leaf_inverse,
    leaf_panel,
    panel_blocks,
    sep_inverse,
    sep_coupling,
):
    yc = ("y", "core")
    zz = ("zh", "zq")
    zq = lax.axis_index("zq")
    zh = lax.axis_index("zh")
    dev = (zh * 4 + zq) * PLANE + lax.axis_index("y") * 2 + lax.axis_index("core")
    place = jnp.stack([zq, zh]).astype(jnp.int32)
    at = jnp.stack([STARTS[k] + dev % (128 >> k) * SEP_DEV for k in range(LEVELS)]).astype(jnp.int32)

    own = jnp.concatenate([sep_inverse, sep_coupling], axis=1)
    quad = lax.all_to_all(jnp.broadcast_to(own, (16,) + own.shape), ("zq", "rhs"), 0, 0)
    quad = jnp.transpose(quad.reshape(4, 4, 8, 1568), (0, 2, 1, 3))
    inv = quad[..., :480].reshape(4, 8, 1920)
    cou = quad[..., 480:].reshape(4, 8, 4352)
    l1 = jnp.concatenate([inv[..., 1024:1536], cou[..., :1024]], axis=2)
    l2 = jnp.concatenate([inv[..., 1536:1792], cou[..., 1024:2560]], axis=2)
    l2 = lax.dynamic_slice_in_dim(l2, zq // 2 * 2, 2, 0)
    l3 = jnp.concatenate([inv[..., 1792:], cou[..., 2560:]], axis=2)
    l3 = lax.dynamic_slice_in_dim(l3, zq, 1, 0)
    l0 = lax.dynamic_slice_in_dim(inv[..., :1024], zq, 1, 0)
    flat = lambda m: jnp.transpose(m, (1, 0, 2)).reshape(8, -1)
    packed = jnp.concatenate([flat(l1), flat(l2), flat(l3), flat(l0)], axis=1)
    path = lax.all_gather(packed, yc, axis=0, tiled=True)

    leaf_forward, pay = call(
        leaf_forward_kernel,
        [f32(SAMPLES, NODES * TILE), f32(SAMPLES, 2048)],
        [
            panel_blocks,
            at,
            leaf_shift,
            sep_shift.T,
            jnp.pad(sep_noise, ((0, 0), (0, 96))),
            leaf_inverse,
            leaf_panel,
        ],
        smem=2,
        scratch=[pltpu.VMEM((ANC, SAMPLES), jnp.float32)],
        flops=50_000_000,
        nbytes=3_000_000,
    )
    pay = lax.all_to_all(pay.reshape(PLANE, GROUP, 2048), yc, 0, 0)
    base, w = call(
        leaf_prepare_kernel,
        [f32(SAMPLES, NODES * TILE), f32(NODES, 64, TILE)],
        [leaf_forward, leaf_noise, leaf_inverse, leaf_panel],
        flops=70_000_000,
        nbytes=4_000_000,
    )
    v = jnp.sum(pay[..., :ANC], axis=0)
    noise = pay[..., ANC : ANC + 32].reshape(PLANE, GROUP, LEVELS, SEP_DEV)
    noise = jnp.transpose(noise, (2, 1, 0, 3)).reshape(LEVELS, GROUP, 128)

    send, g3 = call(
        forward_kernel,
        [f32(8, GROUP, 1792), f32(GROUP, 128)],
        [place, v, noise, path],
        smem=1,
        flops=12_000_000,
        nbytes=6_500_000,
    )
    got = lax.all_to_all(send, zz, 0, 0)
    top_send = call(
        top_kernel, f32(8, GROUP, 1024), [got, noise, path[:, L0_AT:]], flops=2_000_000, nbytes=600_000
    )
    got0 = lax.all_to_all(top_send, zz, 0, 0)
    x = call(
        backward_kernel,
        f32(GROUP, ANC),
        [place, got, got0, g3, path],
        smem=1,
        flops=12_000_000,
        nbytes=6_500_000,
    )
    gathered = lax.all_gather(x, yc, axis=0, tiled=False)

    leaf_out, sep_t = call(
        leaf_backward_kernel,
        [f32(SAMPLES, NODES * TILE), f32(LEVELS * SEP_DEV, SAMPLES)],
        [panel_blocks, at, gathered, base, w],
        smem=2,
        scratch=[pltpu.VMEM((SAMPLES, ANC), jnp.float32), pltpu.VMEM((ANC, SAMPLES), jnp.float32)],
        flops=20_000_000,
        nbytes=2_000_000,
    )
    return leaf_out, sep_t.T


def solution(mesh):
    inner = Mesh(mesh.devices.reshape(2, 4, 8, 2, 4), ("zh", "zq", "y", "core", "rhs"))
    leaf = ("zh", "zq", "y", "core")
    data = P("rhs", leaf)
    rows = P(leaf, "rhs")
    return jax.shard_map(
        body,
        mesh=inner,
        in_specs=(data, data, data, data, P(leaf), P(leaf), P(leaf), rows, rows),
        out_specs=(data, data),
        check_vma=False,
    )
```

```python
import jax
import jax.numpy as jnp
from jax import lax
from jax.experimental import pallas as pl
from jax.experimental.pallas import tpu as pltpu
from jax.sharding import Mesh, PartitionSpec as P

SEP_DEV = 8
LEVELS = 4
NB = 8
ANC = 1920
PLANE = 16
GROUP = 4
SAMPLES = 64
NODES = 16
TILE = 128
STARTS = (0, 1024, 1536, 1792, 1920)
L2_AT = 6144
L3_AT = 9728
L0_AT = 11648
PACK = 12672
RANGES = {"l1": (0, L2_AT), "l2": (L2_AT, L3_AT), "l3": (L3_AT, L0_AT)}

exact = lax.Precision.HIGHEST
MIB = 1024 * 1024


def nn(a, b):
    return lax.dot_general(a, b, (((1,), (0,)), ((), ())), precision=exact, preferred_element_type=jnp.float32)


def nt(a, b):
    return lax.dot_general(a, b, (((1,), (1,)), ((), ())), precision=exact, preferred_element_type=jnp.float32)


def tn(a, b):
    return lax.dot_general(a, b, (((0,), (0,)), ((), ())), precision=exact, preferred_element_type=jnp.float32)


def vspec(n):
    return [pl.BlockSpec(memory_space=pltpu.VMEM)] * n


def call(kernel, outs, ins, smem=0, hbm=0, scratch=(), flops=0, nbytes=0, vmem=12):
    many = isinstance(outs, (list, tuple))
    return pl.pallas_call(
        kernel,
        out_shape=outs,
        in_specs=[pl.BlockSpec(memory_space=pltpu.SMEM)] * smem
        + vspec(len(ins) - smem - hbm)
        + [pl.BlockSpec(memory_space=pl.ANY)] * hbm,
        out_specs=tuple(vspec(len(outs))) if many else vspec(1)[0],
        scratch_shapes=list(scratch),
        compiler_params=pltpu.CompilerParams(vmem_limit_bytes=vmem * MIB),
        cost_estimate=pl.CostEstimate(flops=flops, bytes_accessed=nbytes, transcendentals=0),
    )(*ins)


def f32(*shape):
    return jax.ShapeDtypeStruct(shape, jnp.float32)


def leaf_forward_kernel(blocks, at, shift, sep_t, sep_noise, inverse, panel, lf_out, pay_out, acc):
    acc[...] = jnp.zeros_like(acc)

    def step(n, carry):
        cols = pl.ds(pl.multiple_of(n * TILE, TILE), TILE)
        lf = nt(shift[:, cols], inverse[n])
        lf_out[:, cols] = lf
        pieces = nt(panel[n], lf)
        for b in range(NB):
            rows = pl.ds(pl.multiple_of(blocks[n, b] * SEP_DEV, SEP_DEV), SEP_DEV)
            acc[rows, :] = acc[rows, :] - pieces[b * SEP_DEV : (b + 1) * SEP_DEV, :]
        return carry

    lax.fori_loop(0, NODES, step, 0)
    for k in range(LEVELS):
        rows = pl.ds(pl.multiple_of(at[k], SEP_DEV), SEP_DEV)
        acc[rows, :] = acc[rows, :] + sep_t[k * SEP_DEV : (k + 1) * SEP_DEV, :]
    for c in range(ANC // TILE):
        pay_out[:, c * TILE : (c + 1) * TILE] = acc[c * TILE : (c + 1) * TILE, :].T
    pay_out[:, ANC:] = sep_noise[...]


def leaf_prepare_kernel(lf, noise, inverse, panel, base_out, w_out):
    def step(n, carry):
        cols = pl.ds(pl.multiple_of(n * TILE, TILE), TILE)
        base_out[:, cols] = nn(lf[:, cols] + noise[:, cols], inverse[n])
        w_out[n] = nn(panel[n], inverse[n])
        return carry

    lax.fori_loop(0, NODES, step, 0)


def fetch(source, path, sems, order):
    copies = {}
    for name in order:
        lo, hi = RANGES[name]
        copies[name] = pltpu.make_async_copy(source.at[:, lo:hi], path.at[:, lo:hi], sems.at[order.index(name)])
        copies[name].start()
    return copies


def forward_kernel(place, v, noise, source, send_out, g3_out, path, sems):
    copies = fetch(source, path, sems, ("l3", "l2", "l1"))
    w = v[...]
    copies["l3"].wait()
    g3 = nt(w[:, 1792:], path[:, L3_AT : L3_AT + 128])
    w = w[:, :1792] - nn(g3, path[:, L3_AT + 128 : L0_AT])
    g3_out[...] = g3 + noise[3]
    zq = place[0]
    copies["l2"].wait()
    two = []
    r2 = w[:, 1536:]
    w = w[:, :1536]
    for p in range(2):
        at = L2_AT + p * 1792
        g = nt(r2, path[:, at : at + 256])
        w = w - nn(g, path[:, at + 256 : at + 1792])
        two.append(g + jnp.where(zq % 2 == p, noise[2], 0.0))
    r1 = w[:, 1024:]
    w = w[:, :1024]
    copies["l1"].wait()
    one = []
    for q in range(4):
        at = q * 1536
        g = nt(r1, path[:, at : at + 512])
        w = w - nn(g, path[:, at + 512 : at + 1536])
        one.append(g + jnp.where(zq == q, noise[1], 0.0))
    for d in range(8):
        send_out[d, :, :1024] = w
        for q in range(4):
            send_out[d, :, 1024 + q * 128 : 1152 + q * 128] = one[q]
        for p in range(2):
            send_out[d, :, 1536 + p * 128 : 1664 + p * 128] = two[p]


def top_kernel(got, noise, source, send_out, path, sem):
    copy = pltpu.make_async_copy(source.at[:, L0_AT:], path, sem)
    copy.start()
    r0 = got[0, :, :1024]
    for d in range(1, 8):
        r0 = r0 + got[d, :, :1024]
    copy.wait()
    y0 = nt(r0, path[...]) + noise[0]
    x0 = nn(y0, path[...])
    for d in range(8):
        send_out[d] = x0


def backward_kernel(place, got, got0, g3, source, x_out, path, sems):
    copies = fetch(source, path, sems, ("l1", "l2", "l3"))
    x0 = got0[0]
    for d in range(1, 8):
        x0 = x0 + got0[d]
    x_out[:, :1024] = x0
    z = place[0] + 4 * place[1]
    g1 = jnp.zeros((GROUP, 512), jnp.float32)
    g2 = jnp.zeros((GROUP, 256), jnp.float32)
    for d in range(8):
        g1 = g1 + jnp.where(z // 4 == d // 4, got[d, :, 1024:1536], 0.0)
        g2 = g2 + jnp.where(z // 2 == d // 2, got[d, :, 1536:], 0.0)
    copies["l1"].wait()
    x1 = jnp.zeros((GROUP, 512), jnp.float32)
    for q in range(4):
        at = q * 1536
        y = g1[:, q * 128 : (q + 1) * 128] - nt(x0, path[:, at + 512 : at + 1536])
        x1 = x1 + nn(y, path[:, at : at + 512])
    x_out[:, 1024:1536] = x1
    copies["l2"].wait()
    x2 = jnp.zeros((GROUP, 256), jnp.float32)
    for p in range(2):
        at = L2_AT + p * 1792
        y = g2[:, p * 128 : (p + 1) * 128] - nt(x_out[:, :1536], path[:, at + 256 : at + 1792])
        x2 = x2 + nn(y, path[:, at : at + 256])
    x_out[:, 1536:1792] = x2
    copies["l3"].wait()
    y = g3[...] - nt(x_out[:, :1792], path[:, L3_AT + 128 : L0_AT])
    x_out[:, 1792:] = nn(y, path[:, L3_AT : L3_AT + 128])


def leaf_backward_kernel(blocks, at, x, base, w, leaf_out, sep_out, rows_s, cols_s):
    for g in range(PLANE):
        rows_s[g * GROUP : (g + 1) * GROUP, :] = x[g]
    for c in range(ANC // TILE):
        cols_s[c * TILE : (c + 1) * TILE, :] = rows_s[:, c * TILE : (c + 1) * TILE].T
    for k in range(LEVELS):
        rows = pl.ds(pl.multiple_of(at[k], SEP_DEV), SEP_DEV)
        sep_out[k * SEP_DEV : (k + 1) * SEP_DEV, :] = cols_s[rows, :]

    def step(n, carry):
        cols = pl.ds(pl.multiple_of(n * TILE, TILE), TILE)
        picked = jnp.concatenate(
            [cols_s[pl.ds(pl.multiple_of(blocks[n, b] * SEP_DEV, SEP_DEV), SEP_DEV), :] for b in range(NB)],
            axis=0,
        )
        leaf_out[:, cols] = base[:, cols] - tn(picked, w[n])
        return carry

    lax.fori_loop(0, NODES, step, 0)


def body(
    leaf_shift,
    sep_shift,
    leaf_noise,
    sep_noise,
    leaf_inverse,
    leaf_panel,
    panel_blocks,
    sep_inverse,
    sep_coupling,
):
    yc = ("y", "core")
    zz = ("zh", "zq")
    zq = lax.axis_index("zq")
    zh = lax.axis_index("zh")
    dev = (zh * 4 + zq) * PLANE + lax.axis_index("y") * 2 + lax.axis_index("core")
    place = jnp.stack([zq, zh]).astype(jnp.int32)
    at = jnp.stack([STARTS[k] + dev % (128 >> k) * SEP_DEV for k in range(LEVELS)]).astype(jnp.int32)

    own = jnp.concatenate([sep_inverse, sep_coupling], axis=1)
    quad = lax.all_to_all(jnp.broadcast_to(own, (16,) + own.shape), ("zq", "rhs"), 0, 0)
    first = lax.axis_index("core") == 0
    noise_slot = jnp.concatenate(
        [jnp.where(first, sep_noise, 0.0), jnp.where(first, 0.0, sep_noise), jnp.zeros((SAMPLES, 64), jnp.float32)],
        axis=1,
    )
    leaf_forward, pay = call(
        leaf_forward_kernel,
        [f32(SAMPLES, NODES * TILE), f32(SAMPLES, 2048)],
        [
            panel_blocks,
            at,
            leaf_shift,
            sep_shift.T,
            noise_slot,
            leaf_inverse,
            leaf_panel,
        ],
        smem=2,
        scratch=[pltpu.VMEM((ANC, SAMPLES), jnp.float32)],
        flops=50_000_000,
        nbytes=3_000_000,
    )
    quad, pay = lax.optimization_barrier((quad, pay))
    quad = jnp.transpose(quad.reshape(4, 4, 8, 1568), (0, 2, 1, 3))
    inv = quad[..., :480].reshape(4, 8, 1920)
    cou = quad[..., 480:].reshape(4, 8, 4352)
    l1 = jnp.concatenate([inv[..., 1024:1536], cou[..., :1024]], axis=2)
    l2 = jnp.concatenate([inv[..., 1536:1792], cou[..., 1024:2560]], axis=2)
    l2 = lax.dynamic_slice_in_dim(l2, zq // 2 * 2, 2, 0)
    l3 = jnp.concatenate([inv[..., 1792:], cou[..., 2560:]], axis=2)
    l3 = lax.dynamic_slice_in_dim(l3, zq, 1, 0)
    l0 = lax.dynamic_slice_in_dim(inv[..., :1024], zq, 1, 0)
    flat = lambda m: jnp.transpose(m, (1, 0, 2)).reshape(8, -1)
    packed = jnp.concatenate([flat(l1), flat(l2), flat(l3), flat(l0)], axis=1)
    path = lax.all_gather(packed, yc, axis=0, tiled=True)

    core = lax.axis_index("core")
    pay = pay.reshape(8, 2, GROUP, 2048)
    kept = lax.dynamic_index_in_dim(pay, core, 1, False)
    sent = lax.dynamic_index_in_dim(pay, 1 - core, 1, False)
    pay = kept + lax.ppermute(sent, "core", [(0, 1), (1, 0)])
    pay = lax.all_to_all(pay, "y", 0, 0)
    base, w = call(
        leaf_prepare_kernel,
        [f32(SAMPLES, NODES * TILE), f32(NODES, 64, TILE)],
        [leaf_forward, leaf_noise, leaf_inverse, leaf_panel],
        flops=70_000_000,
        nbytes=4_000_000,
    )
    v = jnp.sum(pay[..., :ANC], axis=0)
    noise = pay[..., ANC : ANC + 64].reshape(8, GROUP, 2, LEVELS, SEP_DEV)
    noise = jnp.transpose(noise, (3, 1, 0, 2, 4)).reshape(LEVELS, GROUP, 128)

    v, base, w = lax.optimization_barrier((v, base, w))
    send, g3 = call(
        forward_kernel,
        [f32(8, GROUP, 1792), f32(GROUP, 128)],
        [place, v, noise, path],
        smem=1,
        hbm=1,
        scratch=[pltpu.VMEM((128, L0_AT), jnp.float32), pltpu.SemaphoreType.DMA((3,))],
        vmem=56,
        flops=12_000_000,
        nbytes=6_500_000,
    )
    got = lax.all_to_all(send, zz, 0, 0)
    top_send = call(
        top_kernel,
        f32(8, GROUP, 1024),
        [got, noise, path],
        hbm=1,
        scratch=[pltpu.VMEM((128, 1024), jnp.float32), pltpu.SemaphoreType.DMA],
        vmem=56,
        flops=2_000_000,
        nbytes=600_000,
    )
    got0 = lax.all_to_all(top_send, zz, 0, 0)
    x = call(
        backward_kernel,
        f32(GROUP, ANC),
        [place, got, got0, g3, path],
        smem=1,
        hbm=1,
        scratch=[pltpu.VMEM((128, L0_AT), jnp.float32), pltpu.SemaphoreType.DMA((3,))],
        vmem=56,
        flops=12_000_000,
        nbytes=6_500_000,
    )
    gathered = lax.all_gather(x, yc, axis=0, tiled=False)

    leaf_out, sep_t = call(
        leaf_backward_kernel,
        [f32(SAMPLES, NODES * TILE), f32(LEVELS * SEP_DEV, SAMPLES)],
        [panel_blocks, at, gathered, base, w],
        smem=2,
        scratch=[pltpu.VMEM((SAMPLES, ANC), jnp.float32), pltpu.VMEM((ANC, SAMPLES), jnp.float32)],
        flops=20_000_000,
        nbytes=2_000_000,
    )
    return leaf_out, sep_t.T


def solution(mesh):
    inner = Mesh(mesh.devices.reshape(2, 4, 8, 2, 4), ("zh", "zq", "y", "core", "rhs"))
    leaf = ("zh", "zq", "y", "core")
    data = P("rhs", leaf)
    rows = P(leaf, "rhs")
    return jax.shard_map(
        body,
        mesh=inner,
        in_specs=(data, data, data, data, P(leaf), P(leaf), P(leaf), rows, rows),
        out_specs=(data, data),
        check_vma=False,
    )
```

```python
import jax
import jax.numpy as jnp
from jax import lax
from jax.experimental import pallas as pl
from jax.experimental.pallas import tpu as pltpu
from jax.sharding import Mesh, PartitionSpec as P

SEP_DEV = 8
LEVELS = 4
NB = 8
ANC = 1920
PLANE = 16
GROUP = 4
SAMPLES = 64
NODES = 16
TILE = 128
STARTS = (0, 1024, 1536, 1792, 1920)
L2_AT = 6144
L3_AT = 9728
L0_AT = 11648
PACK = 12672
RANGES = {"l1": (0, L2_AT), "l2": (L2_AT, L3_AT), "l3": (L3_AT, L0_AT)}

exact = lax.Precision.HIGHEST
MIB = 1024 * 1024


def nn(a, b):
    return lax.dot_general(a, b, (((1,), (0,)), ((), ())), precision=exact, preferred_element_type=jnp.float32)


def nt(a, b):
    return lax.dot_general(a, b, (((1,), (1,)), ((), ())), precision=exact, preferred_element_type=jnp.float32)


def tn(a, b):
    return lax.dot_general(a, b, (((0,), (0,)), ((), ())), precision=exact, preferred_element_type=jnp.float32)


def vspec(n):
    return [pl.BlockSpec(memory_space=pltpu.VMEM)] * n


def call(kernel, outs, ins, smem=0, hbm=0, scratch=(), flops=0, nbytes=0, vmem=12):
    many = isinstance(outs, (list, tuple))
    return pl.pallas_call(
        kernel,
        out_shape=outs,
        in_specs=[pl.BlockSpec(memory_space=pltpu.SMEM)] * smem
        + vspec(len(ins) - smem - hbm)
        + [pl.BlockSpec(memory_space=pl.ANY)] * hbm,
        out_specs=tuple(vspec(len(outs))) if many else vspec(1)[0],
        scratch_shapes=list(scratch),
        compiler_params=pltpu.CompilerParams(vmem_limit_bytes=vmem * MIB),
        cost_estimate=pl.CostEstimate(flops=flops, bytes_accessed=nbytes, transcendentals=0),
    )(*ins)


def f32(*shape):
    return jax.ShapeDtypeStruct(shape, jnp.float32)


def copies_kernel(inverse, coupling, out):
    for d in range(16):
        out[d, :, :480] = inverse[...]
        out[d, :, 480:] = coupling[...]


def pack_kernel(place, quad, out):
    def rows_of(plane):
        parts = [quad[plane * 4 + x] for x in range(4)]
        inv = jnp.concatenate([p[:, :480] for p in parts], axis=1)
        cou = jnp.concatenate([p[:, 480:] for p in parts], axis=1)
        return inv, cou

    for q in range(4):
        inv, cou = rows_of(q)
        out[:, q * 1536 : q * 1536 + 512] = inv[:, 1024:1536]
        out[:, q * 1536 + 512 : (q + 1) * 1536] = cou[:, :1024]
    pair = place[0] // 2 * 2
    for p in range(2):
        inv, cou = rows_of(pair + p)
        at = L2_AT + p * 1792
        out[:, at : at + 256] = inv[:, 1536:1792]
        out[:, at + 256 : at + 1792] = cou[:, 1024:2560]
    inv, cou = rows_of(place[0])
    out[:, L3_AT : L3_AT + 128] = inv[:, 1792:]
    out[:, L3_AT + 128 : L0_AT] = cou[:, 2560:]
    out[:, L0_AT:] = inv[:, :1024]


def leaf_forward_kernel(blocks, at, shift, sep_t, sep_noise, inverse, panel, lf_out, pay_out, acc):
    acc[...] = jnp.zeros_like(acc)

    def step(n, carry):
        cols = pl.ds(pl.multiple_of(n * TILE, TILE), TILE)
        lf = nt(shift[:, cols], inverse[n])
        lf_out[:, cols] = lf
        pieces = nt(panel[n], lf)
        for b in range(NB):
            rows = pl.ds(pl.multiple_of(blocks[n, b] * SEP_DEV, SEP_DEV), SEP_DEV)
            acc[rows, :] = acc[rows, :] - pieces[b * SEP_DEV : (b + 1) * SEP_DEV, :]
        return carry

    lax.fori_loop(0, NODES, step, 0)
    for k in range(LEVELS):
        rows = pl.ds(pl.multiple_of(at[k], SEP_DEV), SEP_DEV)
        acc[rows, :] = acc[rows, :] + sep_t[k * SEP_DEV : (k + 1) * SEP_DEV, :]
    for c in range(ANC // TILE):
        pay_out[:, c * TILE : (c + 1) * TILE] = acc[c * TILE : (c + 1) * TILE, :].T
    pay_out[:, ANC:] = sep_noise[...]


def leaf_prepare_kernel(lf, noise, inverse, panel, base_out, w_out):
    def step(n, carry):
        cols = pl.ds(pl.multiple_of(n * TILE, TILE), TILE)
        base_out[:, cols] = nn(lf[:, cols] + noise[:, cols], inverse[n])
        w_out[n] = nn(panel[n], inverse[n])
        return carry

    lax.fori_loop(0, NODES, step, 0)


def fetch(source, path, sems, order):
    copies = {}
    for name in order:
        lo, hi = RANGES[name]
        copies[name] = pltpu.make_async_copy(source.at[:, lo:hi], path.at[:, lo:hi], sems.at[order.index(name)])
        copies[name].start()
    return copies


def forward_kernel(place, v, noise, source, send_out, g3_out, path, sems):
    copies = fetch(source, path, sems, ("l3", "l2", "l1"))
    w = v[...]
    copies["l3"].wait()
    g3 = nt(w[:, 1792:], path[:, L3_AT : L3_AT + 128])
    w = w[:, :1792] - nn(g3, path[:, L3_AT + 128 : L0_AT])
    g3_out[...] = g3 + noise[3]
    zq = place[0]
    copies["l2"].wait()
    two = []
    r2 = w[:, 1536:]
    w = w[:, :1536]
    for p in range(2):
        at = L2_AT + p * 1792
        g = nt(r2, path[:, at : at + 256])
        w = w - nn(g, path[:, at + 256 : at + 1792])
        two.append(g + jnp.where(zq % 2 == p, noise[2], 0.0))
    r1 = w[:, 1024:]
    w = w[:, :1024]
    copies["l1"].wait()
    one = []
    for q in range(4):
        at = q * 1536
        g = nt(r1, path[:, at : at + 512])
        w = w - nn(g, path[:, at + 512 : at + 1536])
        one.append(g + jnp.where(zq == q, noise[1], 0.0))
    for d in range(8):
        send_out[d, :, :1024] = w
        for q in range(4):
            send_out[d, :, 1024 + q * 128 : 1152 + q * 128] = one[q]
        for p in range(2):
            send_out[d, :, 1536 + p * 128 : 1664 + p * 128] = two[p]


def top_kernel(got, noise, source, send_out, path, sem):
    copy = pltpu.make_async_copy(source.at[:, L0_AT:], path, sem)
    copy.start()
    r0 = got[0, :, :1024]
    for d in range(1, 8):
        r0 = r0 + got[d, :, :1024]
    copy.wait()
    y0 = nt(r0, path[...]) + noise[0]
    x0 = nn(y0, path[...])
    for d in range(8):
        send_out[d] = x0


def backward_kernel(place, got, got0, g3, source, x_out, path, sems):
    copies = fetch(source, path, sems, ("l1", "l2", "l3"))
    x0 = got0[0]
    for d in range(1, 8):
        x0 = x0 + got0[d]
    x_out[:, :1024] = x0
    z = place[0] + 4 * place[1]
    g1 = jnp.zeros((GROUP, 512), jnp.float32)
    g2 = jnp.zeros((GROUP, 256), jnp.float32)
    for d in range(8):
        g1 = g1 + jnp.where(z // 4 == d // 4, got[d, :, 1024:1536], 0.0)
        g2 = g2 + jnp.where(z // 2 == d // 2, got[d, :, 1536:], 0.0)
    copies["l1"].wait()
    x1 = jnp.zeros((GROUP, 512), jnp.float32)
    for q in range(4):
        at = q * 1536
        y = g1[:, q * 128 : (q + 1) * 128] - nt(x0, path[:, at + 512 : at + 1536])
        x1 = x1 + nn(y, path[:, at : at + 512])
    x_out[:, 1024:1536] = x1
    copies["l2"].wait()
    x2 = jnp.zeros((GROUP, 256), jnp.float32)
    for p in range(2):
        at = L2_AT + p * 1792
        y = g2[:, p * 128 : (p + 1) * 128] - nt(x_out[:, :1536], path[:, at + 256 : at + 1792])
        x2 = x2 + nn(y, path[:, at : at + 256])
    x_out[:, 1536:1792] = x2
    copies["l3"].wait()
    y = g3[...] - nt(x_out[:, :1792], path[:, L3_AT + 128 : L0_AT])
    x_out[:, 1792:] = nn(y, path[:, L3_AT : L3_AT + 128])


def leaf_backward_kernel(blocks, at, x, base, w, leaf_out, sep_out, rows_s, cols_s):
    for g in range(PLANE):
        rows_s[g * GROUP : (g + 1) * GROUP, :] = x[g]
    for c in range(ANC // TILE):
        cols_s[c * TILE : (c + 1) * TILE, :] = rows_s[:, c * TILE : (c + 1) * TILE].T
    for k in range(LEVELS):
        rows = pl.ds(pl.multiple_of(at[k], SEP_DEV), SEP_DEV)
        sep_out[k * SEP_DEV : (k + 1) * SEP_DEV, :] = cols_s[rows, :]

    def step(n, carry):
        cols = pl.ds(pl.multiple_of(n * TILE, TILE), TILE)
        picked = jnp.concatenate(
            [cols_s[pl.ds(pl.multiple_of(blocks[n, b] * SEP_DEV, SEP_DEV), SEP_DEV), :] for b in range(NB)],
            axis=0,
        )
        leaf_out[:, cols] = base[:, cols] - tn(picked, w[n])
        return carry

    lax.fori_loop(0, NODES, step, 0)


def body(
    leaf_shift,
    sep_shift,
    leaf_noise,
    sep_noise,
    leaf_inverse,
    leaf_panel,
    panel_blocks,
    sep_inverse,
    sep_coupling,
):
    yc = ("y", "core")
    zz = ("zh", "zq")
    zq = lax.axis_index("zq")
    zh = lax.axis_index("zh")
    dev = (zh * 4 + zq) * PLANE + lax.axis_index("y") * 2 + lax.axis_index("core")
    place = jnp.stack([zq, zh]).astype(jnp.int32)
    at = jnp.stack([STARTS[k] + dev % (128 >> k) * SEP_DEV for k in range(LEVELS)]).astype(jnp.int32)

    copies = call(copies_kernel, f32(16, 8, 1568), [sep_inverse, sep_coupling], nbytes=900_000)
    quad = lax.all_to_all(copies, ("zq", "rhs"), 0, 0)
    first = lax.axis_index("core") == 0
    noise_slot = jnp.concatenate(
        [jnp.where(first, sep_noise, 0.0), jnp.where(first, 0.0, sep_noise), jnp.zeros((SAMPLES, 64), jnp.float32)],
        axis=1,
    )
    leaf_forward, pay = call(
        leaf_forward_kernel,
        [f32(SAMPLES, NODES * TILE), f32(SAMPLES, 2048)],
        [
            panel_blocks,
            at,
            leaf_shift,
            sep_shift.T,
            noise_slot,
            leaf_inverse,
            leaf_panel,
        ],
        smem=2,
        scratch=[pltpu.VMEM((ANC, SAMPLES), jnp.float32)],
        flops=50_000_000,
        nbytes=3_000_000,
    )
    quad, pay = lax.optimization_barrier((quad, pay))
    packed = call(pack_kernel, f32(8, PACK), [place, quad], smem=1, nbytes=1_500_000)
    path = lax.all_gather(packed, yc, axis=0, tiled=True)

    core = lax.axis_index("core")
    pay = pay.reshape(8, 2, GROUP, 2048)
    kept = lax.dynamic_index_in_dim(pay, core, 1, False)
    sent = lax.dynamic_index_in_dim(pay, 1 - core, 1, False)
    pay = kept + lax.ppermute(sent, "core", [(0, 1), (1, 0)])
    pay = lax.all_to_all(pay, "y", 0, 0)
    base, w = call(
        leaf_prepare_kernel,
        [f32(SAMPLES, NODES * TILE), f32(NODES, 64, TILE)],
        [leaf_forward, leaf_noise, leaf_inverse, leaf_panel],
        flops=70_000_000,
        nbytes=4_000_000,
    )
    v = jnp.sum(pay[..., :ANC], axis=0)
    noise = pay[..., ANC : ANC + 64].reshape(8, GROUP, 2, LEVELS, SEP_DEV)
    noise = jnp.transpose(noise, (3, 1, 0, 2, 4)).reshape(LEVELS, GROUP, 128)

    v, base, w = lax.optimization_barrier((v, base, w))
    send, g3 = call(
        forward_kernel,
        [f32(8, GROUP, 1792), f32(GROUP, 128)],
        [place, v, noise, path],
        smem=1,
        hbm=1,
        scratch=[pltpu.VMEM((128, L0_AT), jnp.float32), pltpu.SemaphoreType.DMA((3,))],
        vmem=48,
        flops=12_000_000,
        nbytes=6_500_000,
    )
    got = lax.all_to_all(send, zz, 0, 0)
    top_send = call(
        top_kernel,
        f32(8, GROUP, 1024),
        [got, noise, path],
        hbm=1,
        scratch=[pltpu.VMEM((128, 1024), jnp.float32), pltpu.SemaphoreType.DMA],
        vmem=48,
        flops=2_000_000,
        nbytes=600_000,
    )
    got0 = lax.all_to_all(top_send, zz, 0, 0)
    x = call(
        backward_kernel,
        f32(GROUP, ANC),
        [place, got, got0, g3, path],
        smem=1,
        hbm=1,
        scratch=[pltpu.VMEM((128, L0_AT), jnp.float32), pltpu.SemaphoreType.DMA((3,))],
        vmem=48,
        flops=12_000_000,
        nbytes=6_500_000,
    )
    gathered = lax.all_gather(x, yc, axis=0, tiled=False)

    leaf_out, sep_t = call(
        leaf_backward_kernel,
        [f32(SAMPLES, NODES * TILE), f32(LEVELS * SEP_DEV, SAMPLES)],
        [panel_blocks, at, gathered, base, w],
        smem=2,
        scratch=[pltpu.VMEM((SAMPLES, ANC), jnp.float32), pltpu.VMEM((ANC, SAMPLES), jnp.float32)],
        flops=20_000_000,
        nbytes=2_000_000,
    )
    return leaf_out, sep_t.T


def solution(mesh):
    inner = Mesh(mesh.devices.reshape(2, 4, 8, 2, 4), ("zh", "zq", "y", "core", "rhs"))
    leaf = ("zh", "zq", "y", "core")
    data = P("rhs", leaf)
    rows = P(leaf, "rhs")
    return jax.shard_map(
        body,
        mesh=inner,
        in_specs=(data, data, data, data, P(leaf), P(leaf), P(leaf), rows, rows),
        out_specs=(data, data),
        check_vma=False,
    )
```

```python
import jax
import jax.numpy as jnp
from jax import lax
from jax.experimental import pallas as pl
from jax.experimental.pallas import tpu as pltpu
from jax.sharding import Mesh, PartitionSpec as P

SEP_DEV = 8
LEVELS = 4
NB = 8
ANC = 1920
PLANE = 16
GROUP = 4
SAMPLES = 64
NODES = 16
TILE = 128
STARTS = (0, 1024, 1536, 1792, 1920)
L2_AT = 6144
L3_AT = 9728
L0_AT = 11648
PACK = 12672
RANGES = {"l1": (0, L2_AT), "l2": (L2_AT, L3_AT), "l3": (L3_AT, L0_AT)}

exact = lax.Precision.HIGHEST
MIB = 1024 * 1024


def halves(a):
    high = a.astype(jnp.bfloat16)
    return high, (a - high.astype(jnp.float32)).astype(jnp.bfloat16)


def split_dot(a, b, dims):
    ah, al = halves(a)
    bh, bl = halves(b)
    dot = lambda p, q: lax.dot_general(p, q, (dims, ((), ())), preferred_element_type=jnp.float32)
    return dot(ah, bh) + (dot(ah, bl) + dot(al, bh))


def nn(a, b):
    return split_dot(a, b, ((1,), (0,)))


def nt(a, b):
    return split_dot(a, b, ((1,), (1,)))


def tn(a, b):
    return split_dot(a, b, ((0,), (0,)))


def vspec(n):
    return [pl.BlockSpec(memory_space=pltpu.VMEM)] * n


def call(kernel, outs, ins, smem=0, hbm=0, scratch=(), flops=0, nbytes=0, vmem=12):
    many = isinstance(outs, (list, tuple))
    return pl.pallas_call(
        kernel,
        out_shape=outs,
        in_specs=[pl.BlockSpec(memory_space=pltpu.SMEM)] * smem
        + vspec(len(ins) - smem - hbm)
        + [pl.BlockSpec(memory_space=pl.ANY)] * hbm,
        out_specs=tuple(vspec(len(outs))) if many else vspec(1)[0],
        scratch_shapes=list(scratch),
        compiler_params=pltpu.CompilerParams(vmem_limit_bytes=vmem * MIB),
        cost_estimate=pl.CostEstimate(flops=flops, bytes_accessed=nbytes, transcendentals=0),
    )(*ins)


def f32(*shape):
    return jax.ShapeDtypeStruct(shape, jnp.float32)


def copies_kernel(inverse, coupling, out):
    for d in range(16):
        out[d, :, :480] = inverse[...]
        out[d, :, 480:] = coupling[...]


def pack_kernel(place, quad, out):
    def rows_of(plane):
        parts = [quad[plane * 4 + x] for x in range(4)]
        inv = jnp.concatenate([p[:, :480] for p in parts], axis=1)
        cou = jnp.concatenate([p[:, 480:] for p in parts], axis=1)
        return inv, cou

    for q in range(4):
        inv, cou = rows_of(q)
        out[:, q * 1536 : q * 1536 + 512] = inv[:, 1024:1536]
        out[:, q * 1536 + 512 : (q + 1) * 1536] = cou[:, :1024]
    pair = place[0] // 2 * 2
    for p in range(2):
        inv, cou = rows_of(pair + p)
        at = L2_AT + p * 1792
        out[:, at : at + 256] = inv[:, 1536:1792]
        out[:, at + 256 : at + 1792] = cou[:, 1024:2560]
    inv, cou = rows_of(place[0])
    out[:, L3_AT : L3_AT + 128] = inv[:, 1792:]
    out[:, L3_AT + 128 : L0_AT] = cou[:, 2560:]
    out[:, L0_AT:] = inv[:, :1024]


def leaf_forward_kernel(blocks, at, shift, sep_t, sep_noise, inverse, panel, lf_out, pay_out, acc):
    acc[...] = jnp.zeros_like(acc)

    def step(n, carry):
        cols = pl.ds(pl.multiple_of(n * TILE, TILE), TILE)
        lf = nt(shift[:, cols], inverse[n])
        lf_out[:, cols] = lf
        pieces = nt(panel[n], lf)
        for b in range(NB):
            rows = pl.ds(pl.multiple_of(blocks[n, b] * SEP_DEV, SEP_DEV), SEP_DEV)
            acc[rows, :] = acc[rows, :] - pieces[b * SEP_DEV : (b + 1) * SEP_DEV, :]
        return carry

    lax.fori_loop(0, NODES, step, 0)
    for k in range(LEVELS):
        rows = pl.ds(pl.multiple_of(at[k], SEP_DEV), SEP_DEV)
        acc[rows, :] = acc[rows, :] + sep_t[k * SEP_DEV : (k + 1) * SEP_DEV, :]
    for c in range(ANC // TILE):
        pay_out[:, c * TILE : (c + 1) * TILE] = acc[c * TILE : (c + 1) * TILE, :].T
    pay_out[:, ANC:] = sep_noise[...]


def leaf_prepare_kernel(lf, noise, inverse, panel, base_out, w_out):
    def step(n, carry):
        cols = pl.ds(pl.multiple_of(n * TILE, TILE), TILE)
        base_out[:, cols] = nn(lf[:, cols] + noise[:, cols], inverse[n])
        w_out[n] = nn(panel[n], inverse[n])
        return carry

    lax.fori_loop(0, NODES, step, 0)


def fetch(source, path, sems, order):
    copies = {}
    for name in order:
        lo, hi = RANGES[name]
        copies[name] = pltpu.make_async_copy(source.at[:, lo:hi], path.at[:, lo:hi], sems.at[order.index(name)])
        copies[name].start()
    return copies


def forward_kernel(place, v, noise, source, send_out, g3_out, path, sems):
    copies = fetch(source, path, sems, ("l3", "l2", "l1"))
    w = v[...]
    copies["l3"].wait()
    g3 = nt(w[:, 1792:], path[:, L3_AT : L3_AT + 128])
    w = w[:, :1792] - nn(g3, path[:, L3_AT + 128 : L0_AT])
    g3_out[...] = g3 + noise[3]
    zq = place[0]
    copies["l2"].wait()
    two = []
    r2 = w[:, 1536:]
    w = w[:, :1536]
    for p in range(2):
        at = L2_AT + p * 1792
        g = nt(r2, path[:, at : at + 256])
        w = w - nn(g, path[:, at + 256 : at + 1792])
        two.append(g + jnp.where(zq % 2 == p, noise[2], 0.0))
    r1 = w[:, 1024:]
    w = w[:, :1024]
    copies["l1"].wait()
    one = []
    for q in range(4):
        at = q * 1536
        g = nt(r1, path[:, at : at + 512])
        w = w - nn(g, path[:, at + 512 : at + 1536])
        one.append(g + jnp.where(zq == q, noise[1], 0.0))
    for d in range(8):
        send_out[d, :, :1024] = w
        for q in range(4):
            send_out[d, :, 1024 + q * 128 : 1152 + q * 128] = one[q]
        for p in range(2):
            send_out[d, :, 1536 + p * 128 : 1664 + p * 128] = two[p]


def top_kernel(got, noise, path, send_out):
    r0 = got[0, :, :1024]
    for d in range(1, 8):
        r0 = r0 + got[d, :, :1024]
    y0 = nt(r0, path[...]) + noise[0]
    x0 = nn(y0, path[...])
    for d in range(8):
        send_out[d] = x0


def operator_kernel(source, high_out, low_out, path, found, sems):
    copies = fetch(source, path, sems, ("l1", "l2", "l3"))

    def keep(lo, hi):
        high, low = halves(found[lo:hi, :])
        high_out[lo:hi, :] = high
        low_out[lo:hi, :] = low

    copies["l1"].wait()
    total = None
    for q in range(4):
        at = q * 1536
        term = tn(path[:, at : at + 512], path[:, at + 512 : at + 1536])
        total = term if total is None else total + term
    found[:512, :] = -total
    keep(0, 512)
    copies["l2"].wait()
    total = None
    for p in range(2):
        at = L2_AT + p * 1792
        y = path[:, at + 256 : at + 1280] + nn(path[:, at + 1280 : at + 1792], found[:512, :])
        term = tn(path[:, at : at + 256], y)
        total = term if total is None else total + term
    found[512:768, :] = -total
    keep(512, 768)
    copies["l3"].wait()
    y = path[:, L3_AT + 128 : L3_AT + 1152] + nn(path[:, L3_AT + 1152 : L0_AT], found[:768, :])
    found[768:, :] = -tn(path[:, L3_AT : L3_AT + 128], y)
    keep(768, 896)


def rest_kernel(place, got, g3, source, x_out, path, sems):
    copies = fetch(source, path, sems, ("l1", "l2", "l3"))
    z = place[0] + 4 * place[1]
    g1 = jnp.zeros((GROUP, 512), jnp.float32)
    g2 = jnp.zeros((GROUP, 256), jnp.float32)
    for d in range(8):
        g1 = g1 + jnp.where(z // 4 == d // 4, got[d, :, 1024:1536], 0.0)
        g2 = g2 + jnp.where(z // 2 == d // 2, got[d, :, 1536:], 0.0)
    copies["l1"].wait()
    x1 = jnp.zeros((GROUP, 512), jnp.float32)
    for q in range(4):
        x1 = x1 + nn(g1[:, q * 128 : (q + 1) * 128], path[:, q * 1536 : q * 1536 + 512])
    x_out[:, :512] = x1
    copies["l2"].wait()
    x2 = jnp.zeros((GROUP, 256), jnp.float32)
    for p in range(2):
        at = L2_AT + p * 1792
        y = g2[:, p * 128 : (p + 1) * 128] - nt(x_out[:, :512], path[:, at + 1280 : at + 1792])
        x2 = x2 + nn(y, path[:, at : at + 256])
    x_out[:, 512:768] = x2
    copies["l3"].wait()
    y = g3[...] - nt(x_out[:, :768], path[:, L3_AT + 1152 : L0_AT])
    x_out[:, 768:] = nn(y, path[:, L3_AT : L3_AT + 128])


def backward_kernel(got0, rest, high, low, x_out):
    x0 = got0[0]
    for d in range(1, 8):
        x0 = x0 + got0[d]
    x_out[:, :1024] = x0
    xh, xl = halves(x0)
    dot = lambda p, q: lax.dot_general(p, q[...], (((1,), (1,)), ((), ())), preferred_element_type=jnp.float32)
    x_out[:, 1024:] = rest[...] + (dot(xh, high) + (dot(xh, low) + dot(xl, high)))


def leaf_backward_kernel(blocks, at, x, base, w, leaf_out, sep_out, rows_s, cols_s):
    for g in range(PLANE):
        rows_s[g * GROUP : (g + 1) * GROUP, :] = x[g]
    for c in range(ANC // TILE):
        cols_s[c * TILE : (c + 1) * TILE, :] = rows_s[:, c * TILE : (c + 1) * TILE].T
    for k in range(LEVELS):
        rows = pl.ds(pl.multiple_of(at[k], SEP_DEV), SEP_DEV)
        sep_out[k * SEP_DEV : (k + 1) * SEP_DEV, :] = cols_s[rows, :]

    def step(n, carry):
        cols = pl.ds(pl.multiple_of(n * TILE, TILE), TILE)
        picked = jnp.concatenate(
            [cols_s[pl.ds(pl.multiple_of(blocks[n, b] * SEP_DEV, SEP_DEV), SEP_DEV), :] for b in range(NB)],
            axis=0,
        )
        leaf_out[:, cols] = base[:, cols] - tn(picked, w[n])
        return carry

    lax.fori_loop(0, NODES, step, 0, unroll=4)


def path_scratch(*more):
    return [pltpu.VMEM((128, L0_AT), jnp.float32), *more, pltpu.SemaphoreType.DMA((3,))]


def body(
    leaf_shift,
    sep_shift,
    leaf_noise,
    sep_noise,
    leaf_inverse,
    leaf_panel,
    panel_blocks,
    sep_inverse,
    sep_coupling,
):
    yc = ("y", "core")
    zz = ("zh", "zq")
    zq = lax.axis_index("zq")
    zh = lax.axis_index("zh")
    dev = (zh * 4 + zq) * PLANE + lax.axis_index("y") * 2 + lax.axis_index("core")
    place = jnp.stack([zq, zh]).astype(jnp.int32)
    at = jnp.stack([STARTS[k] + dev % (128 >> k) * SEP_DEV for k in range(LEVELS)]).astype(jnp.int32)

    copies = call(copies_kernel, f32(16, 8, 1568), [sep_inverse, sep_coupling], nbytes=900_000)
    quad = lax.all_to_all(copies, ("zq", "rhs"), 0, 0)
    first = lax.axis_index("core") == 0
    noise_slot = jnp.concatenate(
        [jnp.where(first, sep_noise, 0.0), jnp.where(first, 0.0, sep_noise), jnp.zeros((SAMPLES, 64), jnp.float32)],
        axis=1,
    )
    leaf_forward, pay = call(
        leaf_forward_kernel,
        [f32(SAMPLES, NODES * TILE), f32(SAMPLES, 2048)],
        [
            panel_blocks,
            at,
            leaf_shift,
            sep_shift.T,
            noise_slot,
            leaf_inverse,
            leaf_panel,
        ],
        smem=2,
        scratch=[pltpu.VMEM((ANC, SAMPLES), jnp.float32)],
        flops=50_000_000,
        nbytes=3_000_000,
    )
    quad, pay = lax.optimization_barrier((quad, pay))
    packed = call(pack_kernel, f32(8, PACK), [place, quad], smem=1, nbytes=1_500_000)
    path = lax.all_gather(packed, yc, axis=0, tiled=True)

    core = lax.axis_index("core")
    pay = pay.reshape(8, 2, GROUP, 2048)
    kept = lax.dynamic_index_in_dim(pay, core, 1, False)
    sent = lax.dynamic_index_in_dim(pay, 1 - core, 1, False)
    pay = kept + lax.ppermute(sent, "core", [(0, 1), (1, 0)])
    pay = lax.all_to_all(pay, "y", 0, 0)
    base, w = call(
        leaf_prepare_kernel,
        [f32(SAMPLES, NODES * TILE), f32(NODES, 64, TILE)],
        [leaf_forward, leaf_noise, leaf_inverse, leaf_panel],
        flops=70_000_000,
        nbytes=4_000_000,
    )
    v = jnp.sum(pay[..., :ANC], axis=0)
    noise = pay[..., ANC : ANC + 64].reshape(8, GROUP, 2, LEVELS, SEP_DEV)
    noise = jnp.transpose(noise, (3, 1, 0, 2, 4)).reshape(LEVELS, GROUP, 128)

    v, base, w = lax.optimization_barrier((v, base, w))
    send, g3 = call(
        forward_kernel,
        [f32(8, GROUP, 1792), f32(GROUP, 128)],
        [place, v, noise, path],
        smem=1,
        hbm=1,
        scratch=path_scratch(),
        vmem=48,
        flops=12_000_000,
        nbytes=6_500_000,
    )
    path, send = lax.optimization_barrier((path, send))
    got = lax.all_to_all(send, zz, 0, 0)
    high, low = call(
        operator_kernel,
        [jax.ShapeDtypeStruct((896, 1024), jnp.bfloat16)] * 2,
        [path],
        hbm=1,
        scratch=path_scratch(pltpu.VMEM((896, 1024), jnp.float32)),
        vmem=48,
        flops=3_500_000_000,
        nbytes=10_000_000,
    )
    top_rows = path[:, L0_AT:]
    got, high, low, top_rows = lax.optimization_barrier((got, high, low, top_rows))
    top_send = call(
        top_kernel, f32(8, GROUP, 1024), [got, noise, top_rows], flops=2_000_000, nbytes=600_000, vmem=8
    )
    got0 = lax.all_to_all(top_send, zz, 0, 0)
    rest = call(
        rest_kernel,
        f32(GROUP, 896),
        [place, got, g3, path],
        smem=1,
        hbm=1,
        scratch=path_scratch(),
        vmem=20,
        flops=300_000_000,
        nbytes=6_500_000,
    )
    x = call(
        backward_kernel,
        f32(GROUP, ANC),
        [got0, rest, high, low],
        flops=20_000_000,
        nbytes=4_000_000,
        vmem=16,
    )
    gathered = lax.all_gather(x, yc, axis=0, tiled=False)

    leaf_out, sep_t = call(
        leaf_backward_kernel,
        [f32(SAMPLES, NODES * TILE), f32(LEVELS * SEP_DEV, SAMPLES)],
        [panel_blocks, at, gathered, base, w],
        smem=2,
        scratch=[pltpu.VMEM((SAMPLES, ANC), jnp.float32), pltpu.VMEM((ANC, SAMPLES), jnp.float32)],
        flops=20_000_000,
        nbytes=2_000_000,
    )
    return leaf_out, sep_t.T


def solution(mesh):
    inner = Mesh(mesh.devices.reshape(2, 4, 8, 2, 4), ("zh", "zq", "y", "core", "rhs"))
    leaf = ("zh", "zq", "y", "core")
    data = P("rhs", leaf)
    rows = P(leaf, "rhs")
    return jax.shard_map(
        body,
        mesh=inner,
        in_specs=(data, data, data, data, P(leaf), P(leaf), P(leaf), rows, rows),
        out_specs=(data, data),
        check_vma=False,
    )
```

```python
import jax
import jax.numpy as jnp
from jax import lax
from jax.experimental import pallas as pl
from jax.experimental.pallas import tpu as pltpu
from jax.sharding import Mesh, PartitionSpec as P

SEP_DEV = 8
LEVELS = 4
NB = 8
ANC = 1920
PLANE = 16
GROUP = 4
SAMPLES = 64
NODES = 16
TILE = 128
STARTS = (0, 1024, 1536, 1792, 1920)
L2_AT = 6144
L3_AT = 9728
L0_AT = 11648
PACK = 12672

exact = lax.Precision.HIGHEST
MIB = 1024 * 1024


def halves(a):
    high = a.astype(jnp.bfloat16)
    return high, (a - high.astype(jnp.float32)).astype(jnp.bfloat16)


def split_dot(a, b, dims):
    ah, al = halves(a)
    bh, bl = halves(b)
    dot = lambda p, q: lax.dot_general(p, q, (dims, ((), ())), preferred_element_type=jnp.float32)
    return dot(ah, bh) + (dot(ah, bl) + dot(al, bh))


def nn(a, b):
    return split_dot(a, b, ((1,), (0,)))


def nt(a, b):
    return split_dot(a, b, ((1,), (1,)))


def tn(a, b):
    return split_dot(a, b, ((0,), (0,)))


def vspec(n):
    return [pl.BlockSpec(memory_space=pltpu.VMEM)] * n


def call(kernel, outs, ins, smem=0, hbm=0, scratch=(), flops=0, nbytes=0, vmem=12):
    many = isinstance(outs, (list, tuple))
    return pl.pallas_call(
        kernel,
        out_shape=outs,
        in_specs=[pl.BlockSpec(memory_space=pltpu.SMEM)] * smem
        + vspec(len(ins) - smem - hbm)
        + [pl.BlockSpec(memory_space=pl.ANY)] * hbm,
        out_specs=tuple(vspec(len(outs))) if many else vspec(1)[0],
        scratch_shapes=list(scratch),
        compiler_params=pltpu.CompilerParams(vmem_limit_bytes=vmem * MIB),
        cost_estimate=pl.CostEstimate(flops=flops, bytes_accessed=nbytes, transcendentals=0),
    )(*ins)


def f32(*shape):
    return jax.ShapeDtypeStruct(shape, jnp.float32)


def copies_kernel(inverse, coupling, out):
    for d in range(16):
        out[d, :, :480] = inverse[...]
        out[d, :, 480:] = coupling[...]


def pack_kernel(place, quad, out):
    def rows_of(plane):
        parts = [quad[plane * 4 + x] for x in range(4)]
        inv = jnp.concatenate([p[:, :480] for p in parts], axis=1)
        cou = jnp.concatenate([p[:, 480:] for p in parts], axis=1)
        return inv, cou

    for q in range(4):
        inv, cou = rows_of(q)
        out[:, q * 1536 : q * 1536 + 512] = inv[:, 1024:1536]
        out[:, q * 1536 + 512 : (q + 1) * 1536] = cou[:, :1024]
    pair = place[0] // 2 * 2
    for p in range(2):
        inv, cou = rows_of(pair + p)
        at = L2_AT + p * 1792
        out[:, at : at + 256] = inv[:, 1536:1792]
        out[:, at + 256 : at + 1792] = cou[:, 1024:2560]
    inv, cou = rows_of(place[0])
    out[:, L3_AT : L3_AT + 128] = inv[:, 1792:]
    out[:, L3_AT + 128 : L0_AT] = cou[:, 2560:]
    out[:, L0_AT:] = inv[:, :1024]


def vm(*shape):
    return pltpu.VMEM(shape, jnp.float32)


def bf16(*shape):
    return jax.ShapeDtypeStruct(shape, jnp.bfloat16)


def leaf_forward_kernel(blocks, at, shift, sep_t, sep_noise, inverse, panel, lf_out, pay_out, acc):
    acc[...] = jnp.zeros_like(acc)

    def step(n, carry):
        cols = pl.ds(pl.multiple_of(n * TILE, TILE), TILE)
        lf = nt(shift[:, cols], inverse[n])
        lf_out[:, cols] = lf
        pieces = nt(panel[n], lf)
        for b in range(NB):
            rows = pl.ds(pl.multiple_of(blocks[n, b] * SEP_DEV, SEP_DEV), SEP_DEV)
            acc[rows, :] = acc[rows, :] - pieces[b * SEP_DEV : (b + 1) * SEP_DEV, :]
        return carry

    lax.fori_loop(0, NODES, step, 0)
    for k in range(LEVELS):
        rows = pl.ds(pl.multiple_of(at[k], SEP_DEV), SEP_DEV)
        acc[rows, :] = acc[rows, :] + sep_t[k * SEP_DEV : (k + 1) * SEP_DEV, :]
    for c in range(ANC // TILE):
        pay_out[:, c * TILE : (c + 1) * TILE] = acc[c * TILE : (c + 1) * TILE, :].T
    pay_out[:, ANC:] = sep_noise[...]


def leaf_prepare_kernel(lf, noise, inverse, panel, base_out, w_out):
    def step(n, carry):
        cols = pl.ds(pl.multiple_of(n * TILE, TILE), TILE)
        base_out[:, cols] = nn(lf[:, cols] + noise[:, cols], inverse[n])
        w_out[n] = nn(panel[n], inverse[n])
        return carry

    lax.fori_loop(0, NODES, step, 0)


def fetch(source, sems, target, blocks, at, width, first, used=None):
    used = used or width
    copies = []
    for q in range(blocks):
        copies.append(
            pltpu.make_async_copy(
                source.at[:, at + q * width : at + q * width + used],
                target.at[q * 128 : (q + 1) * 128, :],
                sems.at[first + q],
            )
        )
        copies[q].start()
    return copies


def forward_kernel(place, v, noise, source, send_out, g3_out, l1, l2, l3, sems):
    copies3 = fetch(source, sems, l3, 1, L3_AT, 1920, 0)
    copies2 = fetch(source, sems, l2, 2, L2_AT, 1792, 1)
    copies1 = fetch(source, sems, l1, 4, 0, 1536, 3)
    w = v[...]
    copies3[0].wait()
    g3 = nt(w[:, 1792:], l3[:, :128])
    w = w[:, :1792] - nn(g3, l3[:, 128:])
    g3_out[...] = g3 + noise[3]
    zq = place[0]
    for copy in copies2:
        copy.wait()
    g2 = nt(w[:, 1536:], l2[:, :256])
    w = w[:, :1536] - nn(g2, l2[:, 256:])
    for copy in copies1:
        copy.wait()
    g1 = nt(w[:, 1024:], l1[:, :512])
    w = w[:, :1024] - nn(g1, l1[:, 512:])
    for d in range(8):
        send_out[d, :, :1024] = w
        for q in range(4):
            lanes = slice(q * 128, (q + 1) * 128)
            send_out[d, :, 1024 + q * 128 : 1152 + q * 128] = g1[:, lanes] + jnp.where(zq == q, noise[1], 0.0)
        for p in range(2):
            lanes = slice(p * 128, (p + 1) * 128)
            send_out[d, :, 1536 + p * 128 : 1664 + p * 128] = g2[:, lanes] + jnp.where(zq % 2 == p, noise[2], 0.0)


def top_kernel(got, noise, path, send_out):
    r0 = got[0, :, :1024]
    for d in range(1, 8):
        r0 = r0 + got[d, :, :1024]
    y0 = nt(r0, path[...]) + noise[0]
    x0 = nn(y0, path[...])
    for d in range(8):
        send_out[d] = x0


def operator_kernel(source, map_out, l1, sems):
    for copy in fetch(source, sems, l1, 4, 0, 1536, 0):
        copy.wait()
    found = -tn(l1[:, :512], l1[:, 512:])
    map_out[...] = found


def lower_kernel(place, got, g3, upper, source, x_out, found, inv1, l2, l3, sems):
    copies = fetch(source, sems, inv1, 4, 0, 1536, 3, 512)
    copies += fetch(source, sems, l2, 2, L2_AT, 1792, 1)
    copies += fetch(source, sems, l3, 1, L3_AT, 1920, 0)
    z = place[0] + 4 * place[1]
    g1 = jnp.zeros((GROUP, 512), jnp.float32)
    g2 = jnp.zeros((GROUP, 256), jnp.float32)
    for d in range(8):
        g1 = g1 + jnp.where(z // 4 == d // 4, got[d, :, 1024:1536], 0.0)
        g2 = g2 + jnp.where(z // 2 == d // 2, got[d, :, 1536:], 0.0)
    for copy in copies:
        copy.wait()
    x1 = nn(g1, inv1[...])
    x_out[:, :512] = x1
    x2 = nn(g2 - nt(x1, l2[:, 1280:]), l2[:, :256])
    x_out[:, 512:768] = x2
    x_out[:, 768:] = nn(g3[...] - nt(x_out[:, :768], l3[:, 1152:]), l3[:, :128])
    y = l2[:, 256:1280] + nn(l2[:, 1280:], upper[...])
    found[:256, :] = -tn(l2[:, :256], y)
    y = l3[:, 128:1152] + nn(l3[:, 1152:1664], upper[...]) + nn(l3[:, 1664:], found[:256, :])
    found[256:, :] = -tn(l3[:, :128], y)


def backward_kernel(got0, rest, upper, lower, x_out):
    x0 = got0[0]
    for d in range(1, 8):
        x0 = x0 + got0[d]
    x_out[:, :1024] = x0
    x_out[:, 1024:1536] = rest[:, :512] + nt(x0, upper[...])
    x_out[:, 1536:] = rest[:, 512:] + nt(x0, lower[...])


def leaf_backward_kernel(blocks, at, x, base, w, leaf_out, sep_out, rows_s, cols_s):
    for g in range(PLANE):
        rows_s[g * GROUP : (g + 1) * GROUP, :] = x[g]
    for c in range(ANC // TILE):
        cols_s[c * TILE : (c + 1) * TILE, :] = rows_s[:, c * TILE : (c + 1) * TILE].T
    for k in range(LEVELS):
        rows = pl.ds(pl.multiple_of(at[k], SEP_DEV), SEP_DEV)
        sep_out[k * SEP_DEV : (k + 1) * SEP_DEV, :] = cols_s[rows, :]

    def step(n, carry):
        cols = pl.ds(pl.multiple_of(n * TILE, TILE), TILE)
        picked = jnp.concatenate(
            [cols_s[pl.ds(pl.multiple_of(blocks[n, b] * SEP_DEV, SEP_DEV), SEP_DEV), :] for b in range(NB)],
            axis=0,
        )
        leaf_out[:, cols] = base[:, cols] - tn(picked, w[n])
        return carry

    lax.fori_loop(0, NODES, step, 0, unroll=4)


def body(
    leaf_shift,
    sep_shift,
    leaf_noise,
    sep_noise,
    leaf_inverse,
    leaf_panel,
    panel_blocks,
    sep_inverse,
    sep_coupling,
):
    yc = ("y", "core")
    zz = ("zh", "zq")
    zq = lax.axis_index("zq")
    zh = lax.axis_index("zh")
    dev = (zh * 4 + zq) * PLANE + lax.axis_index("y") * 2 + lax.axis_index("core")
    place = jnp.stack([zq, zh]).astype(jnp.int32)
    at = jnp.stack([STARTS[k] + dev % (128 >> k) * SEP_DEV for k in range(LEVELS)]).astype(jnp.int32)

    copies = call(copies_kernel, f32(16, 8, 1568), [sep_inverse, sep_coupling], nbytes=900_000)
    quad = lax.all_to_all(copies, ("zq", "rhs"), 0, 0)
    first = lax.axis_index("core") == 0
    noise_slot = jnp.concatenate(
        [jnp.where(first, sep_noise, 0.0), jnp.where(first, 0.0, sep_noise), jnp.zeros((SAMPLES, 64), jnp.float32)],
        axis=1,
    )
    leaf_forward, pay = call(
        leaf_forward_kernel,
        [f32(SAMPLES, NODES * TILE), f32(SAMPLES, 2048)],
        [
            panel_blocks,
            at,
            leaf_shift,
            sep_shift.T,
            noise_slot,
            leaf_inverse,
            leaf_panel,
        ],
        smem=2,
        scratch=[pltpu.VMEM((ANC, SAMPLES), jnp.float32)],
        flops=50_000_000,
        nbytes=3_000_000,
    )
    quad, pay = lax.optimization_barrier((quad, pay))
    packed = call(pack_kernel, f32(8, PACK), [place, quad], smem=1, nbytes=1_500_000)
    path = lax.all_gather(packed, yc, axis=0, tiled=True)

    core = lax.axis_index("core")
    pay = pay.reshape(8, 2, GROUP, 2048)
    kept = lax.dynamic_index_in_dim(pay, core, 1, False)
    sent = lax.dynamic_index_in_dim(pay, 1 - core, 1, False)
    pay = kept + lax.ppermute(sent, "core", [(0, 1), (1, 0)])
    pay = lax.all_to_all(pay, "y", 0, 0)
    base, w = call(
        leaf_prepare_kernel,
        [f32(SAMPLES, NODES * TILE), f32(NODES, 64, TILE)],
        [leaf_forward, leaf_noise, leaf_inverse, leaf_panel],
        flops=70_000_000,
        nbytes=4_000_000,
    )
    v = jnp.sum(pay[..., :ANC], axis=0)
    noise = pay[..., ANC : ANC + 64].reshape(8, GROUP, 2, LEVELS, SEP_DEV)
    noise = jnp.transpose(noise, (3, 1, 0, 2, 4)).reshape(LEVELS, GROUP, 128)

    v, base, w = lax.optimization_barrier((v, base, w))
    send, g3 = call(
        forward_kernel,
        [f32(8, GROUP, 1792), f32(GROUP, 128)],
        [place, v, noise, path],
        smem=1,
        hbm=1,
        scratch=[vm(512, 1536), vm(256, 1792), vm(128, 1920), pltpu.SemaphoreType.DMA((7,))],
        vmem=48,
        flops=12_000_000,
        nbytes=6_500_000,
    )
    path, send = lax.optimization_barrier((path, send))
    got = lax.all_to_all(send, zz, 0, 0)
    upper = call(
        operator_kernel,
        f32(512, 1024),
        [path],
        hbm=1,
        scratch=[vm(512, 1536), pltpu.SemaphoreType.DMA((4,))],
        vmem=48,
        flops=1_600_000_000,
        nbytes=10_000_000,
    )
    top_rows = path[:, L0_AT:]
    got, upper, top_rows = lax.optimization_barrier((got, upper, top_rows))
    top_send = call(
        top_kernel, f32(8, GROUP, 1024), [got, noise, top_rows], flops=2_000_000, nbytes=600_000, vmem=8
    )
    got0 = lax.all_to_all(top_send, zz, 0, 0)
    rest, lower = call(
        lower_kernel,
        [f32(GROUP, 896), f32(384, 1024)],
        [place, got, g3, upper, path],
        smem=1,
        hbm=1,
        scratch=[vm(512, 512), vm(256, 1792), vm(128, 1920), pltpu.SemaphoreType.DMA((7,))],
        vmem=48,
        flops=2_200_000_000,
        nbytes=10_000_000,
    )
    x = call(
        backward_kernel,
        f32(GROUP, ANC),
        [got0, rest, upper, lower],
        flops=20_000_000,
        nbytes=4_000_000,
        vmem=16,
    )
    gathered = lax.all_gather(x, yc, axis=0, tiled=False)

    leaf_out, sep_t = call(
        leaf_backward_kernel,
        [f32(SAMPLES, NODES * TILE), f32(LEVELS * SEP_DEV, SAMPLES)],
        [panel_blocks, at, gathered, base, w],
        smem=2,
        scratch=[pltpu.VMEM((SAMPLES, ANC), jnp.float32), pltpu.VMEM((ANC, SAMPLES), jnp.float32)],
        flops=20_000_000,
        nbytes=2_000_000,
    )
    return leaf_out, sep_t.T


def solution(mesh):
    inner = Mesh(mesh.devices.reshape(2, 4, 8, 2, 4), ("zh", "zq", "y", "core", "rhs"))
    leaf = ("zh", "zq", "y", "core")
    data = P("rhs", leaf)
    rows = P(leaf, "rhs")
    return jax.shard_map(
        body,
        mesh=inner,
        in_specs=(data, data, data, data, P(leaf), P(leaf), P(leaf), rows, rows),
        out_specs=(data, data),
        check_vma=False,
    )
```

```python
import jax
import jax.numpy as jnp
from jax import lax
from jax.experimental import pallas as pl
from jax.experimental.pallas import tpu as pltpu
from jax.sharding import Mesh, PartitionSpec as P

SEP_DEV = 8
LEVELS = 4
NB = 8
ANC = 1920
PLANE = 16
GROUP = 4
SAMPLES = 64
NODES = 16
TILE = 128
STARTS = (0, 1024, 1536, 1792, 1920)
L2_AT = 6144
L3_AT = 9728
L0_AT = 11648
PACK = 12672

exact = lax.Precision.HIGHEST
MIB = 1024 * 1024


def halves(a):
    high = a.astype(jnp.bfloat16)
    return high, (a - high.astype(jnp.float32)).astype(jnp.bfloat16)


def split_dot(a, b, dims):
    ah, al = halves(a)
    bh, bl = halves(b)
    dot = lambda p, q: lax.dot_general(p, q, (dims, ((), ())), preferred_element_type=jnp.float32)
    return dot(ah, bh) + (dot(ah, bl) + dot(al, bh))


def nn(a, b):
    return split_dot(a, b, ((1,), (0,)))


def nt(a, b):
    return split_dot(a, b, ((1,), (1,)))


def tn(a, b):
    return split_dot(a, b, ((0,), (0,)))


def vspec(n):
    return [pl.BlockSpec(memory_space=pltpu.VMEM)] * n


def call(kernel, outs, ins, smem=0, hbm=0, scratch=(), flops=0, nbytes=0, vmem=12):
    many = isinstance(outs, (list, tuple))
    return pl.pallas_call(
        kernel,
        out_shape=outs,
        in_specs=[pl.BlockSpec(memory_space=pltpu.SMEM)] * smem
        + vspec(len(ins) - smem - hbm)
        + [pl.BlockSpec(memory_space=pl.ANY)] * hbm,
        out_specs=tuple(vspec(len(outs))) if many else vspec(1)[0],
        scratch_shapes=list(scratch),
        compiler_params=pltpu.CompilerParams(vmem_limit_bytes=vmem * MIB),
        cost_estimate=pl.CostEstimate(flops=flops, bytes_accessed=nbytes, transcendentals=0),
    )(*ins)


def f32(*shape):
    return jax.ShapeDtypeStruct(shape, jnp.float32)


def copies_kernel(inverse_in, coupling_in, out, inverse, coupling, sems):
    one = pltpu.make_async_copy(inverse_in, inverse, sems.at[0])
    two = pltpu.make_async_copy(coupling_in, coupling, sems.at[1])
    one.start()
    two.start()
    one.wait()
    two.wait()
    for d in range(16):
        out[d, :, :480] = inverse[...]
        out[d, :, 480:] = coupling[...]


def pack_kernel(place, quad, out):
    def rows_of(plane):
        parts = [quad[plane * 4 + x] for x in range(4)]
        inv = jnp.concatenate([p[:, :480] for p in parts], axis=1)
        cou = jnp.concatenate([p[:, 480:] for p in parts], axis=1)
        return inv, cou

    for q in range(4):
        inv, cou = rows_of(q)
        out[:, q * 1536 : q * 1536 + 512] = inv[:, 1024:1536]
        out[:, q * 1536 + 512 : (q + 1) * 1536] = cou[:, :1024]
    pair = place[0] // 2 * 2
    for p in range(2):
        inv, cou = rows_of(pair + p)
        at = L2_AT + p * 1792
        out[:, at : at + 256] = inv[:, 1536:1792]
        out[:, at + 256 : at + 1792] = cou[:, 1024:2560]
    inv, cou = rows_of(place[0])
    out[:, L3_AT : L3_AT + 128] = inv[:, 1792:]
    out[:, L3_AT + 128 : L0_AT] = cou[:, 2560:]
    out[:, L0_AT:] = inv[:, :1024]


def vm(*shape):
    return pltpu.VMEM(shape, jnp.float32)


def bf16(*shape):
    return jax.ShapeDtypeStruct(shape, jnp.bfloat16)


def leaf_forward_kernel(blocks, at, shift, sep_t, sep_noise, inverse, panel, lf_out, pay_out, acc):
    acc[...] = jnp.zeros_like(acc)

    def step(n, carry):
        cols = pl.ds(pl.multiple_of(n * TILE, TILE), TILE)
        lf = nt(shift[:, cols], inverse[n])
        lf_out[:, cols] = lf
        pieces = nt(panel[n], lf)
        for b in range(NB):
            rows = pl.ds(pl.multiple_of(blocks[n, b] * SEP_DEV, SEP_DEV), SEP_DEV)
            acc[rows, :] = acc[rows, :] - pieces[b * SEP_DEV : (b + 1) * SEP_DEV, :]
        return carry

    lax.fori_loop(0, NODES, step, 0)
    for k in range(LEVELS):
        rows = pl.ds(pl.multiple_of(at[k], SEP_DEV), SEP_DEV)
        acc[rows, :] = acc[rows, :] + sep_t[k * SEP_DEV : (k + 1) * SEP_DEV, :]
    for c in range(ANC // TILE):
        pay_out[:, c * TILE : (c + 1) * TILE] = acc[c * TILE : (c + 1) * TILE, :].T
    pay_out[:, ANC:] = sep_noise[...]


def leaf_prepare_kernel(lf, noise, inverse, panel, base_out, w_out):
    def step(n, carry):
        cols = pl.ds(pl.multiple_of(n * TILE, TILE), TILE)
        base_out[:, cols] = nn(lf[:, cols] + noise[:, cols], inverse[n])
        w_out[n] = nn(panel[n], inverse[n])
        return carry

    lax.fori_loop(0, NODES, step, 0)


def fetch(source, sems, target, blocks, at, width, first, used=None):
    used = used or width
    copies = []
    for q in range(blocks):
        copies.append(
            pltpu.make_async_copy(
                source.at[:, at + q * width : at + q * width + used],
                target.at[q * 128 : (q + 1) * 128, :],
                sems.at[first + q],
            )
        )
        copies[q].start()
    return copies


def forward_kernel(place, v, noise, source, send_out, g3_out, l1, l2, l3, sems):
    copies3 = fetch(source, sems, l3, 1, L3_AT, 1920, 0)
    copies2 = fetch(source, sems, l2, 2, L2_AT, 1792, 1)
    copies1 = fetch(source, sems, l1, 4, 0, 1536, 3)
    w = v[...]
    copies3[0].wait()
    g3 = nt(w[:, 1792:], l3[:, :128])
    w = w[:, :1792] - nn(g3, l3[:, 128:])
    g3_out[...] = g3 + noise[3]
    zq = place[0]
    for copy in copies2:
        copy.wait()
    g2 = nt(w[:, 1536:], l2[:, :256])
    w = w[:, :1536] - nn(g2, l2[:, 256:])
    for copy in copies1:
        copy.wait()
    g1 = nt(w[:, 1024:], l1[:, :512])
    w = w[:, :1024] - nn(g1, l1[:, 512:])
    for d in range(8):
        send_out[d, :, :1024] = w
        for q in range(4):
            lanes = slice(q * 128, (q + 1) * 128)
            send_out[d, :, 1024 + q * 128 : 1152 + q * 128] = g1[:, lanes] + jnp.where(zq == q, noise[1], 0.0)
        for p in range(2):
            lanes = slice(p * 128, (p + 1) * 128)
            send_out[d, :, 1536 + p * 128 : 1664 + p * 128] = g2[:, lanes] + jnp.where(zq % 2 == p, noise[2], 0.0)


def top_kernel(got, noise, path, send_out):
    r0 = got[0, :, :1024]
    for d in range(1, 8):
        r0 = r0 + got[d, :, :1024]
    y0 = nt(r0, path[...]) + noise[0]
    x0 = nn(y0, path[...])
    for d in range(8):
        send_out[d] = x0


def operator_kernel(source, upper, lower, l1, l2, l3, sems):
    copies1 = fetch(source, sems, l1, 4, 0, 1536, 3)
    copies2 = fetch(source, sems, l2, 2, L2_AT, 1792, 1)
    copies3 = fetch(source, sems, l3, 1, L3_AT, 1920, 0)
    for copy in copies1:
        copy.wait()
    upper[...] = -tn(l1[:, :512], l1[:, 512:])
    for copy in copies2:
        copy.wait()
    y = l2[:, 256:1280] + nn(l2[:, 1280:], upper[...])
    lower[:256, :] = -tn(l2[:, :256], y)
    copies3[0].wait()
    y = l3[:, 128:1152] + nn(l3[:, 1152:1664], upper[...]) + nn(l3[:, 1664:], lower[:256, :])
    lower[256:, :] = -tn(l3[:, :128], y)


def rest_kernel(place, got, g3, upper, lower, source, x_out, inv1, l2, l3, sems):
    copies = fetch(source, sems, inv1, 4, 0, 1536, 3, 512)
    copies += fetch(source, sems, l2, 2, L2_AT, 1792, 1)
    copies += fetch(source, sems, l3, 1, L3_AT, 1920, 0)
    z = place[0] + 4 * place[1]
    g1 = jnp.zeros((GROUP, 512), jnp.float32)
    g2 = jnp.zeros((GROUP, 256), jnp.float32)
    for d in range(8):
        g1 = g1 + jnp.where(z // 4 == d // 4, got[d, :, 1024:1536], 0.0)
        g2 = g2 + jnp.where(z // 2 == d // 2, got[d, :, 1536:], 0.0)
    for copy in copies:
        copy.wait()
    x1 = nn(g1, inv1[...])
    x_out[:, :512] = x1
    x2 = nn(g2 - nt(x1, l2[:, 1280:]), l2[:, :256])
    x_out[:, 512:768] = x2
    x_out[:, 768:] = nn(g3[...] - nt(x_out[:, :768], l3[:, 1152:]), l3[:, :128])


def backward_kernel(got0, rest, upper, lower, x_out):
    x0 = got0[0]
    for d in range(1, 8):
        x0 = x0 + got0[d]
    x_out[:, :1024] = x0
    x_out[:, 1024:1536] = rest[:, :512] + nt(x0, upper[...])
    x_out[:, 1536:] = rest[:, 512:] + nt(x0, lower[...])


def leaf_backward_kernel(blocks, at, x, base, w, leaf_out, sep_out, rows_s, cols_s):
    for g in range(PLANE):
        rows_s[g * GROUP : (g + 1) * GROUP, :] = x[g]
    for c in range(ANC // TILE):
        cols_s[c * TILE : (c + 1) * TILE, :] = rows_s[:, c * TILE : (c + 1) * TILE].T
    for k in range(LEVELS):
        rows = pl.ds(pl.multiple_of(at[k], SEP_DEV), SEP_DEV)
        sep_out[k * SEP_DEV : (k + 1) * SEP_DEV, :] = cols_s[rows, :]

    def step(n, carry):
        cols = pl.ds(pl.multiple_of(n * TILE, TILE), TILE)
        picked = jnp.concatenate(
            [cols_s[pl.ds(pl.multiple_of(blocks[n, b] * SEP_DEV, SEP_DEV), SEP_DEV), :] for b in range(NB)],
            axis=0,
        )
        leaf_out[:, cols] = base[:, cols] - tn(picked, w[n])
        return carry

    lax.fori_loop(0, NODES, step, 0, unroll=4)


def body(
    leaf_shift,
    sep_shift,
    leaf_noise,
    sep_noise,
    leaf_inverse,
    leaf_panel,
    panel_blocks,
    sep_inverse,
    sep_coupling,
):
    yc = ("y", "core")
    zz = ("zh", "zq")
    zq = lax.axis_index("zq")
    zh = lax.axis_index("zh")
    dev = (zh * 4 + zq) * PLANE + lax.axis_index("y") * 2 + lax.axis_index("core")
    place = jnp.stack([zq, zh]).astype(jnp.int32)
    at = jnp.stack([STARTS[k] + dev % (128 >> k) * SEP_DEV for k in range(LEVELS)]).astype(jnp.int32)

    copies = call(
        copies_kernel,
        f32(16, 8, 1568),
        [sep_inverse, sep_coupling],
        hbm=2,
        scratch=[vm(8, 480), vm(8, 1088), pltpu.SemaphoreType.DMA((2,))],
        nbytes=900_000,
    )
    quad = lax.all_to_all(copies, ("zq", "rhs"), 0, 0)
    first = lax.axis_index("core") == 0
    noise_slot = jnp.concatenate(
        [jnp.where(first, sep_noise, 0.0), jnp.where(first, 0.0, sep_noise), jnp.zeros((SAMPLES, 64), jnp.float32)],
        axis=1,
    )
    leaf_forward, pay = call(
        leaf_forward_kernel,
        [f32(SAMPLES, NODES * TILE), f32(SAMPLES, 2048)],
        [
            panel_blocks,
            at,
            leaf_shift,
            sep_shift.T,
            noise_slot,
            leaf_inverse,
            leaf_panel,
        ],
        smem=2,
        scratch=[pltpu.VMEM((ANC, SAMPLES), jnp.float32)],
        flops=50_000_000,
        nbytes=3_000_000,
    )
    quad, pay = lax.optimization_barrier((quad, pay))
    packed = call(pack_kernel, f32(8, PACK), [place, quad], smem=1, nbytes=1_500_000)
    path = lax.all_gather(packed, yc, axis=0, tiled=True)

    core = lax.axis_index("core")
    pay = pay.reshape(8, 2, GROUP, 2048)
    kept = lax.dynamic_index_in_dim(pay, core, 1, False)
    sent = lax.dynamic_index_in_dim(pay, 1 - core, 1, False)
    pay = kept + lax.ppermute(sent, "core", [(0, 1), (1, 0)])
    pay = lax.all_to_all(pay, "y", 0, 0)
    base, w = call(
        leaf_prepare_kernel,
        [f32(SAMPLES, NODES * TILE), f32(NODES, 64, TILE)],
        [leaf_forward, leaf_noise, leaf_inverse, leaf_panel],
        flops=70_000_000,
        nbytes=4_000_000,
    )
    v = jnp.sum(pay[..., :ANC], axis=0)
    noise = pay[..., ANC : ANC + 64].reshape(8, GROUP, 2, LEVELS, SEP_DEV)
    noise = jnp.transpose(noise, (3, 1, 0, 2, 4)).reshape(LEVELS, GROUP, 128)

    v, base, w = lax.optimization_barrier((v, base, w))
    send, g3 = call(
        forward_kernel,
        [f32(8, GROUP, 1792), f32(GROUP, 128)],
        [place, v, noise, path],
        smem=1,
        hbm=1,
        scratch=[vm(512, 1536), vm(256, 1792), vm(128, 1920), pltpu.SemaphoreType.DMA((7,))],
        vmem=48,
        flops=12_000_000,
        nbytes=6_500_000,
    )
    path, send = lax.optimization_barrier((path, send))
    got = lax.all_to_all(send, zz, 0, 0)
    upper, lower = call(
        operator_kernel,
        [f32(512, 1024), f32(384, 1024)],
        [path],
        hbm=1,
        scratch=[vm(512, 1536), vm(256, 1792), vm(128, 1920), pltpu.SemaphoreType.DMA((7,))],
        vmem=48,
        flops=3_500_000_000,
        nbytes=10_000_000,
    )
    top_rows = path[:, L0_AT:]
    got, upper, lower, top_rows = lax.optimization_barrier((got, upper, lower, top_rows))
    top_send = call(
        top_kernel, f32(8, GROUP, 1024), [got, noise, top_rows], flops=2_000_000, nbytes=600_000, vmem=8
    )
    got0 = lax.all_to_all(top_send, zz, 0, 0)
    rest = call(
        rest_kernel,
        f32(GROUP, 896),
        [place, got, g3, upper, lower, path],
        smem=1,
        hbm=1,
        scratch=[vm(512, 512), vm(256, 1792), vm(128, 1920), pltpu.SemaphoreType.DMA((7,))],
        vmem=48,
        flops=300_000_000,
        nbytes=8_000_000,
    )
    x = call(
        backward_kernel,
        f32(GROUP, ANC),
        [got0, rest, upper, lower],
        flops=20_000_000,
        nbytes=4_000_000,
        vmem=16,
    )
    gathered = lax.all_gather(x, yc, axis=0, tiled=False)

    leaf_out, sep_t = call(
        leaf_backward_kernel,
        [f32(SAMPLES, NODES * TILE), f32(LEVELS * SEP_DEV, SAMPLES)],
        [panel_blocks, at, gathered, base, w],
        smem=2,
        scratch=[pltpu.VMEM((SAMPLES, ANC), jnp.float32), pltpu.VMEM((ANC, SAMPLES), jnp.float32)],
        flops=20_000_000,
        nbytes=2_000_000,
    )
    return leaf_out, sep_t.T


def solution(mesh):
    inner = Mesh(mesh.devices.reshape(2, 4, 8, 2, 4), ("zh", "zq", "y", "core", "rhs"))
    leaf = ("zh", "zq", "y", "core")
    data = P("rhs", leaf)
    rows = P(leaf, "rhs")
    return jax.shard_map(
        body,
        mesh=inner,
        in_specs=(data, data, data, data, P(leaf), P(leaf), P(leaf), rows, rows),
        out_specs=(data, data),
        check_vma=False,
    )
```

```python
import jax
import jax.numpy as jnp
from jax import lax
from jax.experimental import pallas as pl
from jax.experimental.pallas import tpu as pltpu
from jax.sharding import Mesh, PartitionSpec as P

SEP_DEV = 8
LEVELS = 4
NB = 8
ANC = 1920
PLANE = 16
GROUP = 4
SAMPLES = 64
NODES = 16
TILE = 128
STARTS = (0, 1024, 1536, 1792, 1920)
L2_AT = 6144
L3_AT = 9728
L0_AT = 11648
PACK = 12672

exact = lax.Precision.HIGHEST
MIB = 1024 * 1024


def halves(a):
    high = a.astype(jnp.bfloat16)
    return high, (a - high.astype(jnp.float32)).astype(jnp.bfloat16)


def split_dot(a, b, dims):
    ah, al = halves(a)
    bh, bl = halves(b)
    dot = lambda p, q: lax.dot_general(p, q, (dims, ((), ())), preferred_element_type=jnp.float32)
    return dot(ah, bh) + (dot(ah, bl) + dot(al, bh))


def nn(a, b):
    return split_dot(a, b, ((1,), (0,)))


def nt(a, b):
    return split_dot(a, b, ((1,), (1,)))


def tn(a, b):
    return split_dot(a, b, ((0,), (0,)))


def vspec(n):
    return [pl.BlockSpec(memory_space=pltpu.VMEM)] * n


def call(kernel, outs, ins, smem=0, hbm=0, scratch=(), flops=0, nbytes=0, vmem=12):
    many = isinstance(outs, (list, tuple))
    return pl.pallas_call(
        kernel,
        out_shape=outs,
        in_specs=[pl.BlockSpec(memory_space=pltpu.SMEM)] * smem
        + vspec(len(ins) - smem - hbm)
        + [pl.BlockSpec(memory_space=pl.ANY)] * hbm,
        out_specs=tuple(vspec(len(outs))) if many else vspec(1)[0],
        scratch_shapes=list(scratch),
        compiler_params=pltpu.CompilerParams(vmem_limit_bytes=vmem * MIB),
        cost_estimate=pl.CostEstimate(flops=flops, bytes_accessed=nbytes, transcendentals=0),
    )(*ins)


def f32(*shape):
    return jax.ShapeDtypeStruct(shape, jnp.float32)


def copies_kernel(inverse, coupling, out):
    for d in range(16):
        out[d, :, :480] = inverse[...]
        out[d, :, 480:] = coupling[...]


def pack_kernel(place, quad, out):
    def rows_of(plane):
        parts = [quad[plane * 4 + x] for x in range(4)]
        inv = jnp.concatenate([p[:, :480] for p in parts], axis=1)
        cou = jnp.concatenate([p[:, 480:] for p in parts], axis=1)
        return inv, cou

    for q in range(4):
        inv, cou = rows_of(q)
        out[:, q * 1536 : q * 1536 + 512] = inv[:, 1024:1536]
        out[:, q * 1536 + 512 : (q + 1) * 1536] = cou[:, :1024]
    pair = place[0] // 2 * 2
    for p in range(2):
        inv, cou = rows_of(pair + p)
        at = L2_AT + p * 1792
        out[:, at : at + 256] = inv[:, 1536:1792]
        out[:, at + 256 : at + 1792] = cou[:, 1024:2560]
    inv, cou = rows_of(place[0])
    out[:, L3_AT : L3_AT + 128] = inv[:, 1792:]
    out[:, L3_AT + 128 : L0_AT] = cou[:, 2560:]
    out[:, L0_AT:] = inv[:, :1024]


def vm(*shape):
    return pltpu.VMEM(shape, jnp.float32)


def bf16(*shape):
    return jax.ShapeDtypeStruct(shape, jnp.bfloat16)


def leaf_forward_kernel(blocks, at, shift, sep_t, sep_noise, inverse, panel, lf_out, pay_out, acc):
    acc[...] = jnp.zeros_like(acc)

    def step(n, carry):
        cols = pl.ds(pl.multiple_of(n * TILE, TILE), TILE)
        lf = nt(shift[:, cols], inverse[n])
        lf_out[:, cols] = lf
        pieces = nt(panel[n], lf)
        for b in range(NB):
            rows = pl.ds(pl.multiple_of(blocks[n, b] * SEP_DEV, SEP_DEV), SEP_DEV)
            acc[rows, :] = acc[rows, :] - pieces[b * SEP_DEV : (b + 1) * SEP_DEV, :]
        return carry

    lax.fori_loop(0, NODES, step, 0)
    for k in range(LEVELS):
        rows = pl.ds(pl.multiple_of(at[k], SEP_DEV), SEP_DEV)
        acc[rows, :] = acc[rows, :] + sep_t[k * SEP_DEV : (k + 1) * SEP_DEV, :]
    for c in range(ANC // TILE):
        pay_out[:, c * TILE : (c + 1) * TILE] = acc[c * TILE : (c + 1) * TILE, :].T
    pay_out[:, ANC:] = sep_noise[...]


def leaf_prepare_kernel(lf, noise, inverse, panel, base_out, w_out):
    def step(n, carry):
        cols = pl.ds(pl.multiple_of(n * TILE, TILE), TILE)
        base_out[:, cols] = nn(lf[:, cols] + noise[:, cols], inverse[n])
        w_out[n] = nn(panel[n], inverse[n])
        return carry

    lax.fori_loop(0, NODES, step, 0)


def fetch(source, sems, target, blocks, at, width, first, used=None):
    used = used or width
    copies = []
    for q in range(blocks):
        copies.append(
            pltpu.make_async_copy(
                source.at[:, at + q * width : at + q * width + used],
                target.at[q * 128 : (q + 1) * 128, :],
                sems.at[first + q],
            )
        )
        copies[q].start()
    return copies


def forward_kernel(place, v, noise, source, send_out, g3_out, l1, l2, l3, sems):
    copies3 = fetch(source, sems, l3, 1, L3_AT, 1920, 0)
    copies2 = fetch(source, sems, l2, 2, L2_AT, 1792, 1)
    copies1 = fetch(source, sems, l1, 4, 0, 1536, 3)
    w = v[...]
    copies3[0].wait()
    g3 = nt(w[:, 1792:], l3[:, :128])
    w = w[:, :1792] - nn(g3, l3[:, 128:])
    g3_out[...] = g3 + noise[3]
    zq = place[0]
    for copy in copies2:
        copy.wait()
    g2 = nt(w[:, 1536:], l2[:, :256])
    w = w[:, :1536] - nn(g2, l2[:, 256:])
    r1 = w[:, 1024:]
    w = w[:, :1024]
    g1 = []
    for q in range(4):
        copies1[q].wait()
        g1.append(nt(r1, l1[q * 128 : (q + 1) * 128, :512]))
        w = w - nn(g1[q], l1[q * 128 : (q + 1) * 128, 512:])
    for d in range(8):
        send_out[d, :, :1024] = w
        for q in range(4):
            send_out[d, :, 1024 + q * 128 : 1152 + q * 128] = g1[q] + jnp.where(zq == q, noise[1], 0.0)
        for p in range(2):
            lanes = slice(p * 128, (p + 1) * 128)
            send_out[d, :, 1536 + p * 128 : 1664 + p * 128] = g2[:, lanes] + jnp.where(zq % 2 == p, noise[2], 0.0)


def top_kernel(got, noise, path, send_out):
    r0 = got[0, :, :1024]
    for d in range(1, 8):
        r0 = r0 + got[d, :, :1024]
    y0 = nt(r0, path[...]) + noise[0]
    x0 = nn(y0, path[...])
    for d in range(8):
        send_out[d] = x0


def operator_kernel(source, map_out, l1, sems):
    for copy in fetch(source, sems, l1, 4, 0, 1536, 0):
        copy.wait()
    found = -tn(l1[:, :512], l1[:, 512:])
    map_out[...] = found


def lower_kernel(place, got, g3, upper, source, x_out, found, inv1, l2, l3, sems):
    copies = fetch(source, sems, inv1, 4, 0, 1536, 3, 512)
    copies += fetch(source, sems, l2, 2, L2_AT, 1792, 1)
    copies += fetch(source, sems, l3, 1, L3_AT, 1920, 0)
    z = place[0] + 4 * place[1]
    g1 = jnp.zeros((GROUP, 512), jnp.float32)
    g2 = jnp.zeros((GROUP, 256), jnp.float32)
    for d in range(8):
        g1 = g1 + jnp.where(z // 4 == d // 4, got[d, :, 1024:1536], 0.0)
        g2 = g2 + jnp.where(z // 2 == d // 2, got[d, :, 1536:], 0.0)
    for copy in copies:
        copy.wait()
    x1 = nn(g1, inv1[...])
    x_out[:, :512] = x1
    x2 = nn(g2 - nt(x1, l2[:, 1280:]), l2[:, :256])
    x_out[:, 512:768] = x2
    x_out[:, 768:] = nn(g3[...] - nt(x_out[:, :768], l3[:, 1152:]), l3[:, :128])
    y = l2[:, 256:1280] + nn(l2[:, 1280:], upper[...])
    found[:256, :] = -tn(l2[:, :256], y)
    y = l3[:, 128:1152] + nn(l3[:, 1152:1664], upper[...]) + nn(l3[:, 1664:], found[:256, :])
    found[256:, :] = -tn(l3[:, :128], y)


def backward_kernel(got0, rest, upper, lower, x_out):
    x0 = got0[0]
    for d in range(1, 8):
        x0 = x0 + got0[d]
    x1 = rest[:, :512] + nt(x0, upper[...])
    x2 = rest[:, 512:] + nt(x0, lower[...])
    for d in range(8):
        x_out[d, :, :1024] = x0
        x_out[d, :, 1024:1536] = x1
        x_out[d, :, 1536:] = x2


def leaf_backward_kernel(blocks, at, x, base, w, leaf_out, sep_out, rows_s, cols_s):
    for g in range(PLANE):
        rows_s[g * GROUP : (g + 1) * GROUP, :] = x[g % 2, g // 2]
    for c in range(ANC // TILE):
        cols_s[c * TILE : (c + 1) * TILE, :] = rows_s[:, c * TILE : (c + 1) * TILE].T
    for k in range(LEVELS):
        rows = pl.ds(pl.multiple_of(at[k], SEP_DEV), SEP_DEV)
        sep_out[k * SEP_DEV : (k + 1) * SEP_DEV, :] = cols_s[rows, :]

    def step(n, carry):
        cols = pl.ds(pl.multiple_of(n * TILE, TILE), TILE)
        picked = jnp.concatenate(
            [cols_s[pl.ds(pl.multiple_of(blocks[n, b] * SEP_DEV, SEP_DEV), SEP_DEV), :] for b in range(NB)],
            axis=0,
        )
        leaf_out[:, cols] = base[:, cols] - tn(picked, w[n])
        return carry

    lax.fori_loop(0, NODES, step, 0, unroll=4)


def body(
    leaf_shift,
    sep_shift,
    leaf_noise,
    sep_noise,
    leaf_inverse,
    leaf_panel,
    panel_blocks,
    sep_inverse,
    sep_coupling,
):
    yc = ("y", "core")
    zz = ("zh", "zq")
    zq = lax.axis_index("zq")
    zh = lax.axis_index("zh")
    dev = (zh * 4 + zq) * PLANE + lax.axis_index("y") * 2 + lax.axis_index("core")
    place = jnp.stack([zq, zh]).astype(jnp.int32)
    at = jnp.stack([STARTS[k] + dev % (128 >> k) * SEP_DEV for k in range(LEVELS)]).astype(jnp.int32)

    copies = call(copies_kernel, f32(16, 8, 1568), [sep_inverse, sep_coupling], nbytes=900_000)
    quad = lax.all_to_all(copies, ("zq", "rhs"), 0, 0)
    first = lax.axis_index("core") == 0
    noise_slot = jnp.concatenate(
        [jnp.where(first, sep_noise, 0.0), jnp.where(first, 0.0, sep_noise), jnp.zeros((SAMPLES, 64), jnp.float32)],
        axis=1,
    )
    leaf_forward, pay = call(
        leaf_forward_kernel,
        [f32(SAMPLES, NODES * TILE), f32(SAMPLES, 2048)],
        [
            panel_blocks,
            at,
            leaf_shift,
            sep_shift.T,
            noise_slot,
            leaf_inverse,
            leaf_panel,
        ],
        smem=2,
        scratch=[pltpu.VMEM((ANC, SAMPLES), jnp.float32)],
        flops=50_000_000,
        nbytes=3_000_000,
    )
    quad, pay = lax.optimization_barrier((quad, pay))
    packed = call(pack_kernel, f32(8, PACK), [place, quad], smem=1, nbytes=1_500_000)
    path = lax.all_gather(packed, yc, axis=0, tiled=True)

    core = lax.axis_index("core")
    pay = pay.reshape(8, 2, GROUP, 2048)
    kept = lax.dynamic_index_in_dim(pay, core, 1, False)
    sent = lax.dynamic_index_in_dim(pay, 1 - core, 1, False)
    pay = kept + lax.ppermute(sent, "core", [(0, 1), (1, 0)])
    pay = lax.all_to_all(pay, "y", 0, 0)
    base, w = call(
        leaf_prepare_kernel,
        [f32(SAMPLES, NODES * TILE), f32(NODES, 64, TILE)],
        [leaf_forward, leaf_noise, leaf_inverse, leaf_panel],
        flops=70_000_000,
        nbytes=4_000_000,
    )
    v = jnp.sum(pay[..., :ANC], axis=0)
    noise = pay[..., ANC : ANC + 64].reshape(8, GROUP, 2, LEVELS, SEP_DEV)
    noise = jnp.transpose(noise, (3, 1, 0, 2, 4)).reshape(LEVELS, GROUP, 128)

    v, base, w = lax.optimization_barrier((v, base, w))
    send, g3 = call(
        forward_kernel,
        [f32(8, GROUP, 1792), f32(GROUP, 128)],
        [place, v, noise, path],
        smem=1,
        hbm=1,
        scratch=[vm(512, 1536), vm(256, 1792), vm(128, 1920), pltpu.SemaphoreType.DMA((7,))],
        vmem=48,
        flops=12_000_000,
        nbytes=6_500_000,
    )
    path, send = lax.optimization_barrier((path, send))
    got = lax.all_to_all(send, zz, 0, 0)
    upper = call(
        operator_kernel,
        f32(512, 1024),
        [path],
        hbm=1,
        scratch=[vm(512, 1536), pltpu.SemaphoreType.DMA((4,))],
        vmem=48,
        flops=1_600_000_000,
        nbytes=10_000_000,
    )
    top_rows = path[:, L0_AT:]
    got, upper, top_rows = lax.optimization_barrier((got, upper, top_rows))
    top_send = call(
        top_kernel, f32(8, GROUP, 1024), [got, noise, top_rows], flops=2_000_000, nbytes=600_000, vmem=8
    )
    got0 = lax.all_to_all(top_send, zz, 0, 0)
    rest, lower = call(
        lower_kernel,
        [f32(GROUP, 896), f32(384, 1024)],
        [place, got, g3, upper, path],
        smem=1,
        hbm=1,
        scratch=[vm(512, 512), vm(256, 1792), vm(128, 1920), pltpu.SemaphoreType.DMA((7,))],
        vmem=48,
        flops=2_200_000_000,
        nbytes=10_000_000,
    )
    x = call(
        backward_kernel,
        f32(8, GROUP, ANC),
        [got0, rest, upper, lower],
        flops=20_000_000,
        nbytes=4_000_000,
        vmem=16,
    )
    x = lax.all_to_all(x, "y", 0, 0)
    gathered = lax.all_gather(x, "core", axis=0, tiled=False)

    leaf_out, sep_t = call(
        leaf_backward_kernel,
        [f32(SAMPLES, NODES * TILE), f32(LEVELS * SEP_DEV, SAMPLES)],
        [panel_blocks, at, gathered, base, w],
        smem=2,
        scratch=[pltpu.VMEM((SAMPLES, ANC), jnp.float32), pltpu.VMEM((ANC, SAMPLES), jnp.float32)],
        flops=20_000_000,
        nbytes=2_000_000,
    )
    return leaf_out, sep_t.T


def solution(mesh):
    inner = Mesh(mesh.devices.reshape(2, 4, 8, 2, 4), ("zh", "zq", "y", "core", "rhs"))
    leaf = ("zh", "zq", "y", "core")
    data = P("rhs", leaf)
    rows = P(leaf, "rhs")
    return jax.shard_map(
        body,
        mesh=inner,
        in_specs=(data, data, data, data, P(leaf), P(leaf), P(leaf), rows, rows),
        out_specs=(data, data),
        check_vma=False,
    )
```

```python
import jax
import jax.numpy as jnp
from jax import lax
from jax.experimental import pallas as pl
from jax.experimental.pallas import tpu as pltpu
from jax.sharding import Mesh, PartitionSpec as P

SEP_DEV = 8
LEVELS = 4
NB = 8
ANC = 1920
PLANE = 16
GROUP = 4
SAMPLES = 64
NODES = 16
TILE = 128
STARTS = (0, 1024, 1536, 1792, 1920)
L2_AT = 6144
L3_AT = 9728
L0_AT = 11648
PACK = 12672

exact = lax.Precision.HIGHEST
MIB = 1024 * 1024


def halves(a):
    high = a.astype(jnp.bfloat16)
    return high, (a - high.astype(jnp.float32)).astype(jnp.bfloat16)


def split_dot(a, b, dims):
    ah, al = halves(a)
    bh, bl = halves(b)
    dot = lambda p, q: lax.dot_general(p, q, (dims, ((), ())), preferred_element_type=jnp.float32)
    return dot(ah, bh) + (dot(ah, bl) + dot(al, bh))


def nn(a, b):
    return split_dot(a, b, ((1,), (0,)))


def nt(a, b):
    return split_dot(a, b, ((1,), (1,)))


def tn(a, b):
    return split_dot(a, b, ((0,), (0,)))


def vspec(n):
    return [pl.BlockSpec(memory_space=pltpu.VMEM)] * n


def call(kernel, outs, ins, smem=0, hbm=0, scratch=(), flops=0, nbytes=0, vmem=12):
    many = isinstance(outs, (list, tuple))
    return pl.pallas_call(
        kernel,
        out_shape=outs,
        in_specs=[pl.BlockSpec(memory_space=pltpu.SMEM)] * smem
        + vspec(len(ins) - smem - hbm)
        + [pl.BlockSpec(memory_space=pl.ANY)] * hbm,
        out_specs=tuple(vspec(len(outs))) if many else vspec(1)[0],
        scratch_shapes=list(scratch),
        compiler_params=pltpu.CompilerParams(vmem_limit_bytes=vmem * MIB),
        cost_estimate=pl.CostEstimate(flops=flops, bytes_accessed=nbytes, transcendentals=0),
    )(*ins)


def f32(*shape):
    return jax.ShapeDtypeStruct(shape, jnp.float32)


def copies_kernel(inverse, coupling, out):
    for d in range(4):
        out[d, :, :480] = inverse[...]
        out[d, :, 480:] = coupling[...]


def rows_kernel(parts, send_out, own_out):
    inv = jnp.concatenate([parts[x, :, :480] for x in range(4)], axis=1)
    cou = jnp.concatenate([parts[x, :, 480:] for x in range(4)], axis=1)
    for d in range(4):
        send_out[d, :, :512] = inv[:, 1024:1536]
        send_out[d, :, 512:1536] = cou[:, :1024]
        send_out[d, :, 1536:1792] = inv[:, 1536:1792]
        send_out[d, :, 1792:] = cou[:, 1024:2560]
    own_out[:, :128] = inv[:, 1792:]
    own_out[:, 128:1920] = cou[:, 2560:]
    own_out[:, 1920:] = inv[:, :1024]


def pack_kernel(place, quad, own, out):
    for q in range(4):
        out[:, q * 1536 : (q + 1) * 1536] = quad[q, :, :1536]
    pair = place[0] // 2 * 2
    for p in range(2):
        at = L2_AT + p * 1792
        out[:, at : at + 1792] = quad[pair + p, :, 1536:]
    out[:, L3_AT:] = own[...]


def vm(*shape):
    return pltpu.VMEM(shape, jnp.float32)


def bf16(*shape):
    return jax.ShapeDtypeStruct(shape, jnp.bfloat16)


def leaf_forward_kernel(blocks, at, shift, sep_t, sep_noise, inverse, panel, lf_out, pay_out, acc):
    acc[...] = jnp.zeros_like(acc)

    def step(n, carry):
        cols = pl.ds(pl.multiple_of(n * TILE, TILE), TILE)
        lf = nt(shift[:, cols], inverse[n])
        lf_out[:, cols] = lf
        pieces = nt(panel[n], lf)
        for b in range(NB):
            rows = pl.ds(pl.multiple_of(blocks[n, b] * SEP_DEV, SEP_DEV), SEP_DEV)
            acc[rows, :] = acc[rows, :] - pieces[b * SEP_DEV : (b + 1) * SEP_DEV, :]
        return carry

    lax.fori_loop(0, NODES, step, 0)
    for k in range(LEVELS):
        rows = pl.ds(pl.multiple_of(at[k], SEP_DEV), SEP_DEV)
        acc[rows, :] = acc[rows, :] + sep_t[k * SEP_DEV : (k + 1) * SEP_DEV, :]
    for c in range(ANC // TILE):
        pay_out[:, c * TILE : (c + 1) * TILE] = acc[c * TILE : (c + 1) * TILE, :].T
    pay_out[:, ANC:] = sep_noise[...]


def leaf_prepare_kernel(lf, noise, inverse, panel, base_out, w_out):
    def step(n, carry):
        cols = pl.ds(pl.multiple_of(n * TILE, TILE), TILE)
        base_out[:, cols] = nn(lf[:, cols] + noise[:, cols], inverse[n])
        w_out[n] = nn(panel[n], inverse[n])
        return carry

    lax.fori_loop(0, NODES, step, 0)


def fetch(source, sems, target, blocks, at, width, first, used=None):
    used = used or width
    copies = []
    for q in range(blocks):
        copies.append(
            pltpu.make_async_copy(
                source.at[:, at + q * width : at + q * width + used],
                target.at[q * 128 : (q + 1) * 128, :],
                sems.at[first + q],
            )
        )
        copies[q].start()
    return copies


def forward_kernel(place, v, noise, source, send_out, g3_out, l1, l2, l3, sems):
    copies3 = fetch(source, sems, l3, 1, L3_AT, 1920, 0)
    copies2 = fetch(source, sems, l2, 2, L2_AT, 1792, 1)
    copies1 = fetch(source, sems, l1, 4, 0, 1536, 3)
    w = v[...]
    copies3[0].wait()
    g3 = nt(w[:, 1792:], l3[:, :128])
    w = w[:, :1792] - nn(g3, l3[:, 128:])
    g3_out[...] = g3 + noise[3]
    zq = place[0]
    for copy in copies2:
        copy.wait()
    g2 = nt(w[:, 1536:], l2[:, :256])
    w = w[:, :1536] - nn(g2, l2[:, 256:])
    for copy in copies1:
        copy.wait()
    g1 = nt(w[:, 1024:], l1[:, :512])
    w = w[:, :1024] - nn(g1, l1[:, 512:])
    for d in range(8):
        send_out[d, :, :1024] = w
        for q in range(4):
            lanes = slice(q * 128, (q + 1) * 128)
            send_out[d, :, 1024 + q * 128 : 1152 + q * 128] = g1[:, lanes] + jnp.where(zq == q, noise[1], 0.0)
        for p in range(2):
            lanes = slice(p * 128, (p + 1) * 128)
            send_out[d, :, 1536 + p * 128 : 1664 + p * 128] = g2[:, lanes] + jnp.where(zq % 2 == p, noise[2], 0.0)


def top_kernel(got, noise, path, send_out):
    r0 = got[0, :, :1024]
    for d in range(1, 8):
        r0 = r0 + got[d, :, :1024]
    y0 = nt(r0, path[...]) + noise[0]
    x0 = nn(y0, path[...])
    for d in range(8):
        send_out[d] = x0


def operator_kernel(source, map_out, l1, sems):
    for copy in fetch(source, sems, l1, 4, 0, 1536, 0):
        copy.wait()
    found = -tn(l1[:, :512], l1[:, 512:])
    map_out[...] = found


def lower_kernel(place, got, g3, upper, source, x_out, found, inv1, l2, l3, sems):
    copies = fetch(source, sems, inv1, 4, 0, 1536, 3, 512)
    copies += fetch(source, sems, l2, 2, L2_AT, 1792, 1)
    copies += fetch(source, sems, l3, 1, L3_AT, 1920, 0)
    z = place[0] + 4 * place[1]
    g1 = jnp.zeros((GROUP, 512), jnp.float32)
    g2 = jnp.zeros((GROUP, 256), jnp.float32)
    for d in range(8):
        g1 = g1 + jnp.where(z // 4 == d // 4, got[d, :, 1024:1536], 0.0)
        g2 = g2 + jnp.where(z // 2 == d // 2, got[d, :, 1536:], 0.0)
    for copy in copies:
        copy.wait()
    x1 = nn(g1, inv1[...])
    x_out[:, :512] = x1
    x2 = nn(g2 - nt(x1, l2[:, 1280:]), l2[:, :256])
    x_out[:, 512:768] = x2
    x_out[:, 768:] = nn(g3[...] - nt(x_out[:, :768], l3[:, 1152:]), l3[:, :128])
    y = l2[:, 256:1280] + nn(l2[:, 1280:], upper[...])
    found[:256, :] = -tn(l2[:, :256], y)
    y = l3[:, 128:1152] + nn(l3[:, 1152:1664], upper[...]) + nn(l3[:, 1664:], found[:256, :])
    found[256:, :] = -tn(l3[:, :128], y)


def backward_kernel(got0, rest, upper, lower, x_out):
    x0 = got0[0]
    for d in range(1, 8):
        x0 = x0 + got0[d]
    x_out[:, :1024] = x0
    x_out[:, 1024:1536] = rest[:, :512] + nt(x0, upper[...])
    x_out[:, 1536:] = rest[:, 512:] + nt(x0, lower[...])


def leaf_backward_kernel(blocks, at, x, base, w, leaf_out, sep_out, rows_s, cols_s):
    for g in range(PLANE):
        rows_s[g * GROUP : (g + 1) * GROUP, :] = x[g]
    for c in range(ANC // TILE):
        cols_s[c * TILE : (c + 1) * TILE, :] = rows_s[:, c * TILE : (c + 1) * TILE].T
    for k in range(LEVELS):
        rows = pl.ds(pl.multiple_of(at[k], SEP_DEV), SEP_DEV)
        sep_out[k * SEP_DEV : (k + 1) * SEP_DEV, :] = cols_s[rows, :]

    def step(n, carry):
        cols = pl.ds(pl.multiple_of(n * TILE, TILE), TILE)
        picked = jnp.concatenate(
            [cols_s[pl.ds(pl.multiple_of(blocks[n, b] * SEP_DEV, SEP_DEV), SEP_DEV), :] for b in range(NB)],
            axis=0,
        )
        leaf_out[:, cols] = base[:, cols] - tn(picked, w[n])
        return carry

    lax.fori_loop(0, NODES, step, 0, unroll=4)


def body(
    leaf_shift,
    sep_shift,
    leaf_noise,
    sep_noise,
    leaf_inverse,
    leaf_panel,
    panel_blocks,
    sep_inverse,
    sep_coupling,
):
    yc = ("y", "core")
    zz = ("zh", "zq")
    zq = lax.axis_index("zq")
    zh = lax.axis_index("zh")
    dev = (zh * 4 + zq) * PLANE + lax.axis_index("y") * 2 + lax.axis_index("core")
    place = jnp.stack([zq, zh]).astype(jnp.int32)
    at = jnp.stack([STARTS[k] + dev % (128 >> k) * SEP_DEV for k in range(LEVELS)]).astype(jnp.int32)

    copies = call(copies_kernel, f32(4, 8, 1568), [sep_inverse, sep_coupling], nbytes=300_000)
    parts = lax.all_to_all(copies, "rhs", 0, 0)
    pieces, own = call(rows_kernel, [f32(4, 8, 3328), f32(8, 2944)], [parts], nbytes=900_000)
    quad = lax.all_to_all(pieces, "zq", 0, 0)
    first = lax.axis_index("core") == 0
    noise_slot = jnp.concatenate(
        [jnp.where(first, sep_noise, 0.0), jnp.where(first, 0.0, sep_noise), jnp.zeros((SAMPLES, 64), jnp.float32)],
        axis=1,
    )
    leaf_forward, pay = call(
        leaf_forward_kernel,
        [f32(SAMPLES, NODES * TILE), f32(SAMPLES, 2048)],
        [
            panel_blocks,
            at,
            leaf_shift,
            sep_shift.T,
            noise_slot,
            leaf_inverse,
            leaf_panel,
        ],
        smem=2,
        scratch=[pltpu.VMEM((ANC, SAMPLES), jnp.float32)],
        flops=50_000_000,
        nbytes=3_000_000,
    )
    quad, pay = lax.optimization_barrier((quad, pay))
    packed = call(pack_kernel, f32(8, PACK), [place, quad, own], smem=1, nbytes=1_500_000)
    path = lax.all_gather(packed, yc, axis=0, tiled=True)

    core = lax.axis_index("core")
    pay = pay.reshape(8, 2, GROUP, 2048)
    kept = lax.dynamic_index_in_dim(pay, core, 1, False)
    sent = lax.dynamic_index_in_dim(pay, 1 - core, 1, False)
    pay = kept + lax.ppermute(sent, "core", [(0, 1), (1, 0)])
    pay = lax.all_to_all(pay, "y", 0, 0)
    base, w = call(
        leaf_prepare_kernel,
        [f32(SAMPLES, NODES * TILE), f32(NODES, 64, TILE)],
        [leaf_forward, leaf_noise, leaf_inverse, leaf_panel],
        flops=70_000_000,
        nbytes=4_000_000,
    )
    v = jnp.sum(pay[..., :ANC], axis=0)
    noise = pay[..., ANC : ANC + 64].reshape(8, GROUP, 2, LEVELS, SEP_DEV)
    noise = jnp.transpose(noise, (3, 1, 0, 2, 4)).reshape(LEVELS, GROUP, 128)

    v, base, w = lax.optimization_barrier((v, base, w))
    send, g3 = call(
        forward_kernel,
        [f32(8, GROUP, 1792), f32(GROUP, 128)],
        [place, v, noise, path],
        smem=1,
        hbm=1,
        scratch=[vm(512, 1536), vm(256, 1792), vm(128, 1920), pltpu.SemaphoreType.DMA((7,))],
        vmem=48,
        flops=12_000_000,
        nbytes=6_500_000,
    )
    path, send = lax.optimization_barrier((path, send))
    got = lax.all_to_all(send, zz, 0, 0)
    upper = call(
        operator_kernel,
        f32(512, 1024),
        [path],
        hbm=1,
        scratch=[vm(512, 1536), pltpu.SemaphoreType.DMA((4,))],
        vmem=48,
        flops=1_600_000_000,
        nbytes=10_000_000,
    )
    top_rows = path[:, L0_AT:]
    got, upper, top_rows = lax.optimization_barrier((got, upper, top_rows))
    top_send = call(
        top_kernel, f32(8, GROUP, 1024), [got, noise, top_rows], flops=2_000_000, nbytes=600_000, vmem=8
    )
    got0 = lax.all_to_all(top_send, zz, 0, 0)
    rest, lower = call(
        lower_kernel,
        [f32(GROUP, 896), f32(384, 1024)],
        [place, got, g3, upper, path],
        smem=1,
        hbm=1,
        scratch=[vm(512, 512), vm(256, 1792), vm(128, 1920), pltpu.SemaphoreType.DMA((7,))],
        vmem=48,
        flops=2_200_000_000,
        nbytes=10_000_000,
    )
    x = call(
        backward_kernel,
        f32(GROUP, ANC),
        [got0, rest, upper, lower],
        flops=20_000_000,
        nbytes=4_000_000,
        vmem=16,
    )
    gathered = lax.all_gather(x, yc, axis=0, tiled=False)

    leaf_out, sep_t = call(
        leaf_backward_kernel,
        [f32(SAMPLES, NODES * TILE), f32(LEVELS * SEP_DEV, SAMPLES)],
        [panel_blocks, at, gathered, base, w],
        smem=2,
        scratch=[pltpu.VMEM((SAMPLES, ANC), jnp.float32), pltpu.VMEM((ANC, SAMPLES), jnp.float32)],
        flops=20_000_000,
        nbytes=2_000_000,
    )
    return leaf_out, sep_t.T


def solution(mesh):
    inner = Mesh(mesh.devices.reshape(2, 4, 8, 2, 4), ("zh", "zq", "y", "core", "rhs"))
    leaf = ("zh", "zq", "y", "core")
    data = P("rhs", leaf)
    rows = P(leaf, "rhs")
    return jax.shard_map(
        body,
        mesh=inner,
        in_specs=(data, data, data, data, P(leaf), P(leaf), P(leaf), rows, rows),
        out_specs=(data, data),
        check_vma=False,
    )
```

```python
import jax
import jax.numpy as jnp
from jax import lax
from jax.experimental import pallas as pl
from jax.experimental.pallas import tpu as pltpu
from jax.sharding import Mesh, PartitionSpec as P

SEP_DEV = 8
LEVELS = 4
NB = 8
ANC = 1920
PLANE = 16
GROUP = 4
SAMPLES = 64
NODES = 16
TILE = 128
STARTS = (0, 1024, 1536, 1792, 1920)
L2_AT = 6144
L3_AT = 9728
L0_AT = 11648
PACK = 12672

exact = lax.Precision.HIGHEST
MIB = 1024 * 1024


def halves(a):
    high = a.astype(jnp.bfloat16)
    return high, (a - high.astype(jnp.float32)).astype(jnp.bfloat16)


def split_dot(a, b, dims):
    ah, al = halves(a)
    bh, bl = halves(b)
    dot = lambda p, q: lax.dot_general(p, q, (dims, ((), ())), preferred_element_type=jnp.float32)
    return dot(ah, bh) + (dot(ah, bl) + dot(al, bh))


def nn(a, b):
    return split_dot(a, b, ((1,), (0,)))


def nt(a, b):
    return split_dot(a, b, ((1,), (1,)))


def tn(a, b):
    return split_dot(a, b, ((0,), (0,)))


def vspec(n):
    return [pl.BlockSpec(memory_space=pltpu.VMEM)] * n


def call(kernel, outs, ins, smem=0, hbm=0, scratch=(), flops=0, nbytes=0, vmem=12, pin=False):
    many = isinstance(outs, (list, tuple))
    held = len(ins) - hbm if pin else len(ins)
    ins = list(ins[:held]) + [pltpu.with_memory_space_constraint(x, pltpu.HBM) for x in ins[held:]]
    return pl.pallas_call(
        kernel,
        out_shape=outs,
        in_specs=[pl.BlockSpec(memory_space=pltpu.SMEM)] * smem
        + vspec(len(ins) - smem - hbm)
        + [pl.BlockSpec(memory_space=pltpu.HBM if pin else pl.ANY)] * hbm,
        out_specs=tuple(vspec(len(outs))) if many else vspec(1)[0],
        scratch_shapes=list(scratch),
        compiler_params=pltpu.CompilerParams(vmem_limit_bytes=vmem * MIB),
        cost_estimate=pl.CostEstimate(flops=flops, bytes_accessed=nbytes, transcendentals=0),
    )(*ins)


def f32(*shape):
    return jax.ShapeDtypeStruct(shape, jnp.float32)


def copies_kernel(inverse_in, coupling_in, out, inverse, coupling, sems):
    one = pltpu.make_async_copy(inverse_in, inverse, sems.at[0])
    two = pltpu.make_async_copy(coupling_in, coupling, sems.at[1])
    one.start()
    two.start()
    one.wait()
    two.wait()
    for d in range(4):
        out[d, :, :480] = inverse[...]
        out[d, :, 480:] = coupling[...]


def rows_kernel(parts, send_out, own_out):
    inv = jnp.concatenate([parts[x, :, :480] for x in range(4)], axis=1)
    cou = jnp.concatenate([parts[x, :, 480:] for x in range(4)], axis=1)
    for d in range(4):
        send_out[d, :, :512] = inv[:, 1024:1536]
        send_out[d, :, 512:1536] = cou[:, :1024]
        send_out[d, :, 1536:1792] = inv[:, 1536:1792]
        send_out[d, :, 1792:] = cou[:, 1024:2560]
    own_out[:, :128] = inv[:, 1792:]
    own_out[:, 128:1920] = cou[:, 2560:]
    own_out[:, 1920:] = inv[:, :1024]


def pack_kernel(place, quad, own, out):
    for q in range(4):
        out[:, q * 1536 : (q + 1) * 1536] = quad[q, :, :1536]
    pair = place[0] // 2 * 2
    for p in range(2):
        at = L2_AT + p * 1792
        out[:, at : at + 1792] = quad[pair + p, :, 1536:]
    out[:, L3_AT:] = own[...]


def vm(*shape):
    return pltpu.VMEM(shape, jnp.float32)


def bf16(*shape):
    return jax.ShapeDtypeStruct(shape, jnp.bfloat16)


def leaf_forward_kernel(blocks, at, shift, sep_t, sep_noise, inverse, panel, lf_out, pay_out, acc):
    acc[...] = jnp.zeros_like(acc)

    def step(n, carry):
        cols = pl.ds(pl.multiple_of(n * TILE, TILE), TILE)
        lf = nt(shift[:, cols], inverse[n])
        lf_out[:, cols] = lf
        pieces = nt(panel[n], lf)
        for b in range(NB):
            rows = pl.ds(pl.multiple_of(blocks[n, b] * SEP_DEV, SEP_DEV), SEP_DEV)
            acc[rows, :] = acc[rows, :] - pieces[b * SEP_DEV : (b + 1) * SEP_DEV, :]
        return carry

    lax.fori_loop(0, NODES, step, 0)
    for k in range(LEVELS):
        rows = pl.ds(pl.multiple_of(at[k], SEP_DEV), SEP_DEV)
        acc[rows, :] = acc[rows, :] + sep_t[k * SEP_DEV : (k + 1) * SEP_DEV, :]
    for c in range(ANC // TILE):
        pay_out[:, c * TILE : (c + 1) * TILE] = acc[c * TILE : (c + 1) * TILE, :].T
    pay_out[:, ANC:] = sep_noise[...]


def leaf_prepare_kernel(lf, noise, inverse, panel, base_out, w_out):
    def step(n, carry):
        cols = pl.ds(pl.multiple_of(n * TILE, TILE), TILE)
        base_out[:, cols] = nn(lf[:, cols] + noise[:, cols], inverse[n])
        w_out[n] = nn(panel[n], inverse[n])
        return carry

    lax.fori_loop(0, NODES, step, 0)


def fetch(source, sems, target, blocks, at, width, first, used=None):
    used = used or width
    copies = []
    for q in range(blocks):
        copies.append(
            pltpu.make_async_copy(
                source.at[:, at + q * width : at + q * width + used],
                target.at[q * 128 : (q + 1) * 128, :],
                sems.at[first + q],
            )
        )
        copies[q].start()
    return copies


def forward_kernel(place, v, noise, source, send_out, g3_out, l1, l2, l3, sems):
    copies3 = fetch(source, sems, l3, 1, L3_AT, 1920, 0)
    copies2 = fetch(source, sems, l2, 2, L2_AT, 1792, 1)
    copies1 = fetch(source, sems, l1, 4, 0, 1536, 3)
    w = v[...]
    copies3[0].wait()
    g3 = nt(w[:, 1792:], l3[:, :128])
    w = w[:, :1792] - nn(g3, l3[:, 128:])
    g3_out[...] = g3 + noise[3]
    zq = place[0]
    for copy in copies2:
        copy.wait()
    g2 = nt(w[:, 1536:], l2[:, :256])
    w = w[:, :1536] - nn(g2, l2[:, 256:])
    for copy in copies1:
        copy.wait()
    g1 = nt(w[:, 1024:], l1[:, :512])
    w = w[:, :1024] - nn(g1, l1[:, 512:])
    for d in range(8):
        send_out[d, :, :1024] = w
        for q in range(4):
            lanes = slice(q * 128, (q + 1) * 128)
            send_out[d, :, 1024 + q * 128 : 1152 + q * 128] = g1[:, lanes] + jnp.where(zq == q, noise[1], 0.0)
        for p in range(2):
            lanes = slice(p * 128, (p + 1) * 128)
            send_out[d, :, 1536 + p * 128 : 1664 + p * 128] = g2[:, lanes] + jnp.where(zq % 2 == p, noise[2], 0.0)


def top_kernel(got, noise, path, send_out):
    r0 = got[0, :, :1024]
    for d in range(1, 8):
        r0 = r0 + got[d, :, :1024]
    y0 = nt(r0, path[...]) + noise[0]
    x0 = nn(y0, path[...])
    for d in range(8):
        send_out[d] = x0


def operator_kernel(source, map_out, l1, sems):
    for copy in fetch(source, sems, l1, 4, 0, 1536, 0):
        copy.wait()
    found = -tn(l1[:, :512], l1[:, 512:])
    map_out[...] = found


def lower_kernel(place, got, g3, upper, source, x_out, found, inv1, l2, l3, sems):
    copies = fetch(source, sems, inv1, 4, 0, 1536, 3, 512)
    copies += fetch(source, sems, l2, 2, L2_AT, 1792, 1)
    copies += fetch(source, sems, l3, 1, L3_AT, 1920, 0)
    z = place[0] + 4 * place[1]
    g1 = jnp.zeros((GROUP, 512), jnp.float32)
    g2 = jnp.zeros((GROUP, 256), jnp.float32)
    for d in range(8):
        g1 = g1 + jnp.where(z // 4 == d // 4, got[d, :, 1024:1536], 0.0)
        g2 = g2 + jnp.where(z // 2 == d // 2, got[d, :, 1536:], 0.0)
    for copy in copies:
        copy.wait()
    x1 = nn(g1, inv1[...])
    x_out[:, :512] = x1
    x2 = nn(g2 - nt(x1, l2[:, 1280:]), l2[:, :256])
    x_out[:, 512:768] = x2
    x_out[:, 768:] = nn(g3[...] - nt(x_out[:, :768], l3[:, 1152:]), l3[:, :128])
    y = l2[:, 256:1280] + nn(l2[:, 1280:], upper[...])
    found[:256, :] = -tn(l2[:, :256], y)
    y = l3[:, 128:1152] + nn(l3[:, 1152:1664], upper[...]) + nn(l3[:, 1664:], found[:256, :])
    found[256:, :] = -tn(l3[:, :128], y)


def backward_kernel(got0, rest, upper, lower, x_out):
    x0 = got0[0]
    for d in range(1, 8):
        x0 = x0 + got0[d]
    x_out[:, :1024] = x0
    x_out[:, 1024:1536] = rest[:, :512] + nt(x0, upper[...])
    x_out[:, 1536:] = rest[:, 512:] + nt(x0, lower[...])


def leaf_backward_kernel(blocks, at, x, base, w, leaf_out, sep_out, rows_s, cols_s):
    for g in range(PLANE):
        rows_s[g * GROUP : (g + 1) * GROUP, :] = x[g]
    for c in range(ANC // TILE):
        cols_s[c * TILE : (c + 1) * TILE, :] = rows_s[:, c * TILE : (c + 1) * TILE].T
    for k in range(LEVELS):
        rows = pl.ds(pl.multiple_of(at[k], SEP_DEV), SEP_DEV)
        sep_out[k * SEP_DEV : (k + 1) * SEP_DEV, :] = cols_s[rows, :]

    def step(n, carry):
        cols = pl.ds(pl.multiple_of(n * TILE, TILE), TILE)
        picked = jnp.concatenate(
            [cols_s[pl.ds(pl.multiple_of(blocks[n, b] * SEP_DEV, SEP_DEV), SEP_DEV), :] for b in range(NB)],
            axis=0,
        )
        leaf_out[:, cols] = base[:, cols] - tn(picked, w[n])
        return carry

    lax.fori_loop(0, NODES, step, 0, unroll=4)


def body(
    leaf_shift,
    sep_shift,
    leaf_noise,
    sep_noise,
    leaf_inverse,
    leaf_panel,
    panel_blocks,
    sep_inverse,
    sep_coupling,
):
    yc = ("y", "core")
    zz = ("zh", "zq")
    zq = lax.axis_index("zq")
    zh = lax.axis_index("zh")
    dev = (zh * 4 + zq) * PLANE + lax.axis_index("y") * 2 + lax.axis_index("core")
    place = jnp.stack([zq, zh]).astype(jnp.int32)
    at = jnp.stack([STARTS[k] + dev % (128 >> k) * SEP_DEV for k in range(LEVELS)]).astype(jnp.int32)

    copies = call(
        copies_kernel,
        f32(4, 8, 1568),
        [sep_inverse, sep_coupling],
        hbm=2,
        pin=True,
        scratch=[vm(8, 480), vm(8, 1088), pltpu.SemaphoreType.DMA((2,))],
        nbytes=300_000,
    )
    parts = lax.all_to_all(copies, "rhs", 0, 0)
    pieces, own = call(rows_kernel, [f32(4, 8, 3328), f32(8, 2944)], [parts], nbytes=900_000)
    quad = lax.all_to_all(pieces, "zq", 0, 0)
    first = lax.axis_index("core") == 0
    noise_slot = jnp.concatenate(
        [jnp.where(first, sep_noise, 0.0), jnp.where(first, 0.0, sep_noise), jnp.zeros((SAMPLES, 64), jnp.float32)],
        axis=1,
    )
    leaf_forward, pay = call(
        leaf_forward_kernel,
        [f32(SAMPLES, NODES * TILE), f32(SAMPLES, 2048)],
        [
            panel_blocks,
            at,
            leaf_shift,
            sep_shift.T,
            noise_slot,
            leaf_inverse,
            leaf_panel,
        ],
        smem=2,
        scratch=[pltpu.VMEM((ANC, SAMPLES), jnp.float32)],
        flops=50_000_000,
        nbytes=3_000_000,
    )
    quad, pay = lax.optimization_barrier((quad, pay))
    packed = call(pack_kernel, f32(8, PACK), [place, quad, own], smem=1, nbytes=1_500_000)
    path = lax.all_gather(packed, yc, axis=0, tiled=True)

    core = lax.axis_index("core")
    pay = pay.reshape(8, 2, GROUP, 2048)
    kept = lax.dynamic_index_in_dim(pay, core, 1, False)
    sent = lax.dynamic_index_in_dim(pay, 1 - core, 1, False)
    pay = kept + lax.ppermute(sent, "core", [(0, 1), (1, 0)])
    pay = lax.all_to_all(pay, "y", 0, 0)
    base, w = call(
        leaf_prepare_kernel,
        [f32(SAMPLES, NODES * TILE), f32(NODES, 64, TILE)],
        [leaf_forward, leaf_noise, leaf_inverse, leaf_panel],
        flops=70_000_000,
        nbytes=4_000_000,
    )
    v = jnp.sum(pay[..., :ANC], axis=0)
    noise = pay[..., ANC : ANC + 64].reshape(8, GROUP, 2, LEVELS, SEP_DEV)
    noise = jnp.transpose(noise, (3, 1, 0, 2, 4)).reshape(LEVELS, GROUP, 128)

    v, base, w = lax.optimization_barrier((v, base, w))
    send, g3 = call(
        forward_kernel,
        [f32(8, GROUP, 1792), f32(GROUP, 128)],
        [place, v, noise, path],
        smem=1,
        hbm=1,
        scratch=[vm(512, 1536), vm(256, 1792), vm(128, 1920), pltpu.SemaphoreType.DMA((7,))],
        vmem=48,
        flops=12_000_000,
        nbytes=6_500_000,
    )
    path, send = lax.optimization_barrier((path, send))
    got = lax.all_to_all(send, zz, 0, 0)
    upper = call(
        operator_kernel,
        f32(512, 1024),
        [path],
        hbm=1,
        scratch=[vm(512, 1536), pltpu.SemaphoreType.DMA((4,))],
        vmem=48,
        flops=1_600_000_000,
        nbytes=10_000_000,
    )
    top_rows = path[:, L0_AT:]
    got, upper, top_rows = lax.optimization_barrier((got, upper, top_rows))
    top_send = call(
        top_kernel, f32(8, GROUP, 1024), [got, noise, top_rows], flops=2_000_000, nbytes=600_000, vmem=8
    )
    got0 = lax.all_to_all(top_send, zz, 0, 0)
    rest, lower = call(
        lower_kernel,
        [f32(GROUP, 896), f32(384, 1024)],
        [place, got, g3, upper, path],
        smem=1,
        hbm=1,
        scratch=[vm(512, 512), vm(256, 1792), vm(128, 1920), pltpu.SemaphoreType.DMA((7,))],
        vmem=48,
        flops=2_200_000_000,
        nbytes=10_000_000,
    )
    x = call(
        backward_kernel,
        f32(GROUP, ANC),
        [got0, rest, upper, lower],
        flops=20_000_000,
        nbytes=4_000_000,
        vmem=16,
    )
    gathered = lax.all_gather(x, yc, axis=0, tiled=False)

    leaf_out, sep_t = call(
        leaf_backward_kernel,
        [f32(SAMPLES, NODES * TILE), f32(LEVELS * SEP_DEV, SAMPLES)],
        [panel_blocks, at, gathered, base, w],
        smem=2,
        scratch=[pltpu.VMEM((SAMPLES, ANC), jnp.float32), pltpu.VMEM((ANC, SAMPLES), jnp.float32)],
        flops=20_000_000,
        nbytes=2_000_000,
    )
    return leaf_out, sep_t.T


def solution(mesh):
    inner = Mesh(mesh.devices.reshape(2, 4, 8, 2, 4), ("zh", "zq", "y", "core", "rhs"))
    leaf = ("zh", "zq", "y", "core")
    data = P("rhs", leaf)
    rows = P(leaf, "rhs")
    return jax.shard_map(
        body,
        mesh=inner,
        in_specs=(data, data, data, data, P(leaf), P(leaf), P(leaf), rows, rows),
        out_specs=(data, data),
        check_vma=False,
    )
```
